512 devices in a mesh: wide: 128 (over x, z, core), narrow: 4 (over y).
Axes of the slice: x: 4, y: 4, z: 16, core: 2. Of those that a mesh axis runs over, the one named last changes fastest.
Arguments:
- restart: float32 [65536, 1024], P('wide', 'narrow'), may hold values from -0.09 to 0.09
- slab_slot: int32 [16384], P('wide'), may hold values from 0 to 16383, as said below
- block_cols: int32 [1024, 16], replicated, may hold values from 0 to 1023, as said below
- filter_cols: int32 [1024, 16], replicated, may hold values from 0 to 1023, as said below
Outputs:
- squared: float32 [65536, 1024], P('wide', 'narrow')
- updated: float32 [65536, 1024], P('wide', 'narrow')
The draws below stay inside these ranges and needn't reach their ends.
Inputs may be any that keep to these rules, and one draw needn't show every extreme that they name: `slab_slot`: A permutation of all slabs; each aligned block of 128 entries names exactly 128 // 128 slabs of each aligned range of 128 values. `block_cols`: each row i holds 16 distinct block columns c with (c - i) mod 1024 within 8 of 0 either way, i itself among them. `filter_cols`: each row i holds 16 distinct block columns c with (c - i) mod 1024 within 8 of 0 either way, i itself among them.
All inputs are finite; a program needn't handle non-finite values.
Results may differ from the reference program's by a relative error of at most 0.0003.
Values sent between devices are 32-bit elements; how exact they have to be, the bound alone decides.
No kernel may reach another device: no remote copies, remote signals or barrier semaphores. Data moves between devices by JAX's collectives and lax.ppermute only.
A program may use at most 192 MiB of HBM per device.

```python
import jax
import jax.numpy as jnp
from jax import lax

BLOCK = 64
KNZ = 16
JNZ = 16
SLAB = 4
BROWS = 8
NBR = 1024
SLABS_DEV = 128
NSLAB = 16384
N_WIDE = 128


def draw_pattern(key, picks):
    window = 2 * BROWS + 1
    key_rank, key_order = jax.random.split(key)
    scores = jax.random.randint(key_rank, (NBR, window), 0, 1 << 16) * window + jnp.arange(window, dtype=jnp.int32)
    places = jnp.arange(window, dtype=jnp.int32)
    forced = places == BROWS
    scores = scores + jnp.where(forced, 1 << 26, 0).astype(jnp.int32)
    chosen = lax.top_k(scores, picks)[1]
    shuffle = jax.random.randint(key_order, (NBR, picks), 0, 1 << 16) * picks + jnp.arange(picks, dtype=jnp.int32)
    ordering = lax.top_k(shuffle, picks)[1]
    chosen = jnp.take_along_axis(chosen, ordering, axis=1)
    row_index = jnp.arange(NBR, dtype=jnp.int32)[:, None]
    return ((row_index + chosen - BROWS) % NBR).astype(jnp.int32)


def draw_block_cols(key, part):
    key = jax.random.fold_in(key, 3)
    return draw_pattern(key, KNZ)


def draw_filter_cols(key, part):
    key = jax.random.fold_in(key, 5)
    return draw_pattern(key, JNZ)


def draw_slab_slot(key, part):
    key = jax.random.fold_in(key, 11)
    key_shift, key_perm = jax.random.split(key)
    shifts = jax.random.randint(key_shift, (N_WIDE,), 0, N_WIDE)
    entries = jnp.arange(SLABS_DEV, dtype=jnp.int32)
    owners = entries % N_WIDE
    rounds = entries // N_WIDE
    perms = jax.vmap(lambda single: jax.random.permutation(single, SLABS_DEV))(jax.random.split(key_perm, N_WIDE))
    device_index = jnp.arange(N_WIDE, dtype=jnp.int32)[:, None]
    owner_of = owners[perms]
    round_of = rounds[perms]
    position = round_of * N_WIDE + (device_index + shifts[owner_of]) % N_WIDE
    return (owner_of * SLABS_DEV + position).reshape(-1).astype(jnp.int32)


def steps_of(own_key, shape, pieces, low, top_value):
    def one(axis_at, parts):
        draws = jax.random.uniform(jax.random.fold_in(jax.random.fold_in(own_key, 6), axis_at), (parts,), jnp.float32, low / len(pieces), top_value / len(pieces))
        return jnp.repeat(jnp.exp(draws), shape[axis_at] // parts).reshape((-1,) + (1,) * (len(shape) - axis_at - 1))

    level = one(*pieces[0])
    for cut in pieces[1:]:
        level = level * one(*cut)
    return level


def gaussian(key, dims, width, reach, pieces=(), kind=jnp.bfloat16):
    values = width * jax.random.normal(key, dims, jnp.float32)
    if pieces:
        values = values * steps_of(key, dims, pieces, -0.22, 0.18)
    return jnp.clip(values, -reach, reach).astype(kind)


def setup_inputs(seed: int = 0) -> dict:
    arg_keys = jax.random.split(jax.random.key(seed), 5)
    return {
        "restart": gaussian(arg_keys[0], (NSLAB * SLAB, KNZ * BLOCK), 0.015, 0.09, ((0, 128), (1, 4)), jnp.float32),
        "slab_slot": draw_slab_slot(jax.random.fold_in(arg_keys[4], 71), 0),
        "block_cols": draw_block_cols(jax.random.fold_in(arg_keys[4], 71), 0),
        "filter_cols": draw_filter_cols(jax.random.fold_in(arg_keys[4], 71), 0),
    }


def multiply(left_rows, left_cols, right_rows, right_cols, out_cols):
    groups = NBR // BROWS

    def one_group(index):
        start = index * BROWS
        lefts = lax.dynamic_slice_in_dim(left_rows, start, BROWS, 0)
        lcols = lax.dynamic_slice_in_dim(left_cols, start, BROWS, 0)
        wanted = lax.dynamic_slice_in_dim(out_cols, start, BROWS, 0)
        blocks = right_rows[lcols]
        picked = right_cols[lcols]
        matches = (picked[:, :, :, None] == wanted[:, None, None, :]).astype(jnp.float32)
        products = jnp.einsum("iakc,ikcmb->iakmb", lefts, blocks, precision=lax.Precision.HIGHEST)
        return jnp.einsum("iakmb,ikmj->iajb", products, matches, precision=lax.Precision.HIGHEST)

    result = lax.map(one_group, jnp.arange(groups, dtype=jnp.int32))
    return result.reshape(NBR, BLOCK, -1, BLOCK)


def reference(restart, slab_slot, block_cols, filter_cols):
    slabs = restart.reshape(NSLAB, SLAB, KNZ * BLOCK)
    placed = jnp.zeros_like(slabs).at[slab_slot].set(slabs)
    matrix = placed.reshape(NBR, BLOCK, KNZ, BLOCK)
    squared = multiply(matrix, block_cols, matrix, block_cols, filter_cols)
    cubic = multiply(matrix, block_cols, squared, filter_cols, filter_cols)
    keep_mask = (block_cols[:, :, None] == filter_cols[:, None, :]).astype(jnp.float32)
    kept_blocks = jnp.einsum("iakb,ikj->iajb", matrix, keep_mask, precision=lax.Precision.HIGHEST)
    updated = 1.5 * kept_blocks - 0.5 * cubic
    return squared.reshape(NBR * BLOCK, JNZ * BLOCK), updated.reshape(NBR * BLOCK, JNZ * BLOCK)
```

```python
import functools

import jax
import jax.numpy as jnp
from jax import lax
from jax.experimental import pallas as pl
from jax.experimental.pallas import tpu as pltpu
from jax.sharding import PartitionSpec as P

BLOCK = 64
KNZ = 16
JNZ = 16
SLAB = 4
N_WIDE = 128
LAYERS = 4
OWN = 8
NBR = 1024
SLABS = 128
ROWS = OWN * BLOCK
WIDTH = 256
CLASS = 6
CLASS_COLS = CLASS * BLOCK
NEAR = 3 * OWN
HALF = 2 * BLOCK

AT_ROW = 0
AT_SLOT = AT_ROW + OWN * KNZ
AT_KEEP = AT_SLOT + OWN * CLASS
AT_ABS = AT_KEEP + OWN * CLASS
AT_REL = AT_ABS + OWN * JNZ
TABLE = AT_REL + OWN * JNZ

VMEM = pl.BlockSpec(memory_space=pltpu.VMEM)
SMEM = pl.BlockSpec(memory_space=pltpu.SMEM)
PARAMS = pltpu.CompilerParams(vmem_limit_bytes=48 * 1024 * 1024)


def cost(flops, bytes_accessed):
    return pl.CostEstimate(flops=flops, bytes_accessed=bytes_accessed, transcendentals=0)


def f32(*shape):
    return jax.ShapeDtypeStruct(shape, jnp.float32)


def pack_kernel(slot_ref, rows_ref, out_ref):
    low = lax.broadcasted_iota(jnp.int32, (8, 128), 0) < SLAB
    for pair in range(SLABS // 2):
        left = rows_ref[8 * pair : 8 * pair + 8, 0:128]
        right = rows_ref[8 * pair : 8 * pair + 8, 128:256]
        first = jnp.where(low, left, pltpu.roll(right, SLAB, 0))
        second = jnp.where(low, pltpu.roll(left, SLAB, 0), right)
        for which, tile in ((0, first), (1, second)):
            slot = slot_ref[2 * pair + which]
            target = slot >> 7
            out_ref[target, 0:8] = tile.reshape(8, 1, 128)
            out_ref[target, 8] = jnp.full((1, 128), (slot & 127).astype(jnp.float32))


def unpack_kernel(position_ref, arrived_ref, rows_ref, tiles):
    for source in range(N_WIDE):
        tiles[position_ref[source]] = arrived_ref[source, 0:8].reshape(8, 128)
    low = lax.broadcasted_iota(jnp.int32, (8, 128), 0) < SLAB
    for pair in range(SLABS // 2):
        first = tiles[2 * pair]
        second = tiles[2 * pair + 1]
        rows_ref[8 * pair : 8 * pair + 8, 0:128] = jnp.where(low, first, pltpu.roll(second, SLAB, 0))
        rows_ref[8 * pair : 8 * pair + 8, 128:256] = jnp.where(low, pltpu.roll(first, SLAB, 0), second)


def pick_pair(source, rows, slot_a, slot_b, none, first_half):
    def one(slot, half):
        there = slot != none
        safe = jnp.where(there, slot, 0)
        block = source[safe >> 1, rows, :]
        turned = pltpu.roll(block, BLOCK, 1)
        same = (safe & 1) == half
        return jnp.where(there, jnp.where(same, block, turned), 0.0)

    return jnp.where(first_half, one(slot_a, 0), one(slot_b, 1))


def class_kernel(table_ref, s0, s1, s2, s3, own_ref, to_right, to_left, chunks):
    for r, shard in enumerate((s0, s1, s2, s3)):
        chunks[2 * r] = shard[:, 0:128]
        chunks[2 * r + 1] = shard[:, 128:256]
    first_half = lax.broadcasted_iota(jnp.int32, (BLOCK, HALF), 1) < BLOCK
    for i in range(OWN):
        rows = slice(i * BLOCK, (i + 1) * BLOCK)
        for q in range(CLASS // 2):
            at = AT_SLOT + i * CLASS + 2 * q
            block = pick_pair(chunks, rows, table_ref[at], table_ref[at + 1], KNZ, first_half)
            own_ref[rows, q * 128 : (q + 1) * 128] = block
            if q > 0:
                to_right[rows, (q - 1) * 128 : q * 128] = block
            if q < 2:
                to_left[rows, q * 128 : (q + 1) * 128] = block


def split(x):
    high = x.astype(jnp.bfloat16)
    return high, (x - high.astype(jnp.float32)).astype(jnp.bfloat16)


def product(table_ref, shards, own_ref, from_left, from_right, right_high, right_low, finish):
    empty = jnp.zeros((ROWS, 128), jnp.bfloat16)
    for source, row, col in ((from_left, 0, 0), (own_ref, ROWS, 0), (from_right, 2 * ROWS, 128)):
        width = source.shape[1]
        high, low = split(source[...])
        right_high[row : row + ROWS, col : col + width] = high
        right_low[row : row + ROWS, col : col + width] = low
    for store in (right_high, right_low):
        store[0:ROWS, WIDTH:CLASS_COLS] = empty
        store[2 * ROWS : 3 * ROWS, 0:128] = empty
    dot = functools.partial(jnp.dot, preferred_element_type=jnp.float32)
    for i in range(OWN):
        rows = slice(i * BLOCK, (i + 1) * BLOCK)
        total = jnp.zeros((BLOCK, CLASS_COLS), jnp.float32)
        for r, shard in enumerate(shards):
            high, low = split(shard[rows, :])
            places = [
                pl.ds(pl.multiple_of(table_ref[AT_ROW + i * KNZ + 4 * r + k] * BLOCK, BLOCK), BLOCK)
                for k in range(KNZ // LAYERS)
            ]
            weight_high = jnp.concatenate([right_high[p, :] for p in places], axis=0)
            weight_low = jnp.concatenate([right_low[p, :] for p in places], axis=0)
            both = dot(jnp.concatenate([high, low], axis=0), weight_high)
            total = total + both[:BLOCK] + both[BLOCK:] + dot(high, weight_low)
        finish(i, rows, total)


def square_kernel(
    table_ref, s0, s1, s2, s3, own_ref, from_left, from_right, square_ref, to_right, to_left, slots_ref, right_high, right_low, chunks
):
    first_half = lax.broadcasted_iota(jnp.int32, (BLOCK, HALF), 1) < BLOCK

    def finish(i, rows, total):
        for q in range(CLASS // 2):
            at = AT_KEEP + i * CLASS + 2 * q
            keep = jnp.where(first_half, table_ref[at], table_ref[at + 1]) != 0
            block = jnp.where(keep, total[:, q * 128 : (q + 1) * 128], 0.0)
            chunks[q, rows, :] = block
            square_ref[rows, q * 128 : (q + 1) * 128] = block
            if q > 0:
                to_right[rows, (q - 1) * 128 : q * 128] = block
            if q < 2:
                to_left[rows, q * 128 : (q + 1) * 128] = block
        for c in range(JNZ // 2):
            at = AT_ABS + i * JNZ + 2 * c
            block = pick_pair(chunks, rows, table_ref[at], table_ref[at + 1], -1, first_half)
            slots_ref[c // 2, rows, (c % 2) * 128 : (c % 2 + 1) * 128] = block

    product(table_ref, (s0, s1, s2, s3), own_ref, from_left, from_right, right_high, right_low, finish)


def cubic_kernel(
    table_ref, s0, s1, s2, s3, own_ref, from_left, from_right, keep_ref, o0, o1, o2, o3, right_high, right_low, chunks
):
    first_half = lax.broadcasted_iota(jnp.int32, (BLOCK, HALF), 1) < BLOCK
    outs = (o0, o1, o2, o3)

    def finish(i, rows, total):
        for q in range(CLASS // 2):
            cols = slice(q * 128, (q + 1) * 128)
            chunks[q, rows, :] = 1.5 * keep_ref[rows, cols] - 0.5 * total[:, cols]
        for c in range(JNZ // 2):
            at = AT_REL + i * JNZ + 2 * c
            block = pick_pair(chunks, rows, table_ref[at], table_ref[at + 1], -1, first_half)
            outs[c // 2][rows, (c % 2) * 128 : (c % 2 + 1) * 128] = block

    product(table_ref, (s0, s1, s2, s3), own_ref, from_left, from_right, right_high, right_low, finish)


RIGHT = [
    pltpu.VMEM((NEAR * BLOCK, CLASS_COLS), jnp.bfloat16),
    pltpu.VMEM((NEAR * BLOCK, CLASS_COLS), jnp.bfloat16),
    pltpu.VMEM((CLASS // 2, ROWS, HALF), jnp.float32),
]


def shift(x, axis, by):
    count = lax.axis_size(axis)
    return lax.ppermute(x, axis, [(i, (i + by) % count) for i in range(count)])


def tables(block_cols, filter_cols, wide_index, layer):
    first_row = wide_index * OWN
    base = first_row - OWN

    def own(cols):
        mine = lax.dynamic_slice_in_dim(cols, first_row, OWN, 0)
        mine = (mine - base) & (NBR - 1)
        turned = lax.dynamic_slice_in_dim(jnp.concatenate([mine, mine], axis=1), layer * (KNZ // LAYERS), KNZ, 1)
        return mine, turned

    _, cols = own(block_cols)
    kept, kept_turned = own(filter_cols)
    places = layer + LAYERS * jnp.arange(CLASS, dtype=jnp.int32)
    slots = jnp.arange(KNZ, dtype=jnp.int32)
    slot = jnp.min(jnp.where(cols[:, None, :] == places[None, :, None], slots, KNZ), axis=2)
    keep = jnp.max((kept[:, None, :] == places[None, :, None]).astype(jnp.int32), axis=2)

    def source(filters):
        return jnp.where((filters - layer) & (LAYERS - 1) == 0, (filters - layer) >> 2, -1)

    return jnp.concatenate([part.reshape(-1) for part in (cols, slot, keep, source(kept), source(kept_turned))])


def local(restart, slab_slot, block_cols, filter_cols):
    wide_index = lax.axis_index("wide")
    layer = lax.axis_index("narrow")
    table = tables(block_cols, filter_cols, wide_index, layer)

    packed = pl.pallas_call(
        pack_kernel,
        out_shape=f32(N_WIDE, 9, 1, 128),
        in_specs=[SMEM, VMEM],
        out_specs=VMEM,
        compiler_params=PARAMS,
        cost_estimate=cost(0, 1 << 20),
        name="pack",
    )(slab_slot, restart)
    arrived = lax.all_to_all(packed, "wide", split_axis=0, concat_axis=0, tiled=True)
    position = arrived[:, 8, 0, 0].astype(jnp.int32)
    mine = pl.pallas_call(
        unpack_kernel,
        out_shape=f32(ROWS, WIDTH),
        in_specs=[SMEM, VMEM],
        out_specs=VMEM,
        scratch_shapes=[pltpu.VMEM((SLABS, 8, 128), jnp.float32)],
        compiler_params=PARAMS,
        cost_estimate=cost(0, 1 << 20),
        name="unpack",
    )(position, arrived)
    shards = (mine, shift(mine, "narrow", -1), shift(mine, "narrow", -2), shift(mine, "narrow", -3))

    half = f32(ROWS, WIDTH)
    whole = f32(ROWS, CLASS_COLS)
    own, to_right, to_left = pl.pallas_call(
        class_kernel,
        out_shape=(whole, half, half),
        in_specs=[SMEM] + [VMEM] * 4,
        out_specs=(VMEM,) * 3,
        scratch_shapes=[pltpu.VMEM((2 * LAYERS, ROWS, HALF), jnp.float32)],
        compiler_params=PARAMS,
        cost_estimate=cost(0, 4 << 20),
        name="columns_of_class",
    )(table, *shards)
    from_left = shift(to_right, "wide", 1)
    from_right = shift(to_left, "wide", -1)

    flops = 2 * 3 * ROWS * KNZ * BLOCK * CLASS_COLS
    square, to_right, to_left, square_slots = pl.pallas_call(
        square_kernel,
        out_shape=(whole, half, half, f32(LAYERS, ROWS, WIDTH)),
        in_specs=[SMEM] + [VMEM] * 7,
        out_specs=(VMEM,) * 4,
        scratch_shapes=RIGHT,
        compiler_params=PARAMS,
        cost_estimate=cost(flops, 8 << 20),
        name="square",
    )(table, *shards, own, from_left, from_right)
    squared = lax.psum_scatter(square_slots, "narrow", scatter_dimension=0)
    from_left = shift(to_right, "wide", 1)
    from_right = shift(to_left, "wide", -1)

    parts = pl.pallas_call(
        cubic_kernel,
        out_shape=(half,) * 4,
        in_specs=[SMEM] + [VMEM] * 8,
        out_specs=(VMEM,) * 4,
        scratch_shapes=RIGHT,
        compiler_params=PARAMS,
        cost_estimate=cost(flops, 8 << 20),
        name="cubic",
    )(table, *shards, square, from_left, from_right, own)
    updated = parts[0] + shift(parts[1], "narrow", 1) + shift(parts[2], "narrow", 2) + shift(parts[3], "narrow", 3)
    return (squared, updated)


def solution(mesh):
    placed = (P("wide", "narrow"), P("wide"), P(), P())
    return jax.shard_map(
        local,
        mesh=mesh,
        in_specs=placed,
        out_specs=(P("wide", "narrow"), P("wide", "narrow")),
        check_vma=False,
    )
```

```python
import functools

import jax
import jax.numpy as jnp
from jax import lax
from jax.experimental import pallas as pl
from jax.experimental.pallas import tpu as pltpu
from jax.sharding import PartitionSpec as P

BLOCK = 64
KNZ = 16
JNZ = 16
SLAB = 4
N_WIDE = 128
LAYERS = 4
OWN = 8
NBR = 1024
SLABS = 128
ROWS = OWN * BLOCK
WIDTH = 256
CLASS = 6
CLASS_COLS = CLASS * BLOCK
NEAR = 3 * OWN
HALF = 2 * BLOCK

AT_ROW = 0
AT_SLOT = AT_ROW + OWN * KNZ
AT_KEEP = AT_SLOT + OWN * CLASS
AT_ABS = AT_KEEP + OWN * CLASS
AT_REL = AT_ABS + OWN * JNZ
TABLE = AT_REL + OWN * JNZ

VMEM = pl.BlockSpec(memory_space=pltpu.VMEM)
SMEM = pl.BlockSpec(memory_space=pltpu.SMEM)
PARAMS = pltpu.CompilerParams(vmem_limit_bytes=24 * 1024 * 1024)


def cost(flops, bytes_accessed):
    return pl.CostEstimate(flops=flops, bytes_accessed=bytes_accessed, transcendentals=0)


def f32(*shape):
    return jax.ShapeDtypeStruct(shape, jnp.float32)


def pack_kernel(slot_ref, rows_ref, out_ref):
    low = lax.broadcasted_iota(jnp.int32, (8, 128), 0) < SLAB
    for pair in range(SLABS // 2):
        left = rows_ref[8 * pair : 8 * pair + 8, 0:128]
        right = rows_ref[8 * pair : 8 * pair + 8, 128:256]
        first = jnp.where(low, left, pltpu.roll(right, SLAB, 0))
        second = jnp.where(low, pltpu.roll(left, SLAB, 0), right)
        for which, tile in ((0, first), (1, second)):
            slot = slot_ref[2 * pair + which]
            target = slot >> 7
            out_ref[target, 0:8] = tile.reshape(8, 1, 128)
            out_ref[target, 8] = jnp.full((1, 128), (slot & 127).astype(jnp.float32))


def unpack_kernel(position_ref, arrived_ref, rows_ref, tiles):
    for source in range(N_WIDE):
        tiles[position_ref[source]] = arrived_ref[source, 0:8].reshape(8, 128)
    low = lax.broadcasted_iota(jnp.int32, (8, 128), 0) < SLAB
    for pair in range(SLABS // 2):
        first = tiles[2 * pair]
        second = tiles[2 * pair + 1]
        rows_ref[8 * pair : 8 * pair + 8, 0:128] = jnp.where(low, first, pltpu.roll(second, SLAB, 0))
        rows_ref[8 * pair : 8 * pair + 8, 128:256] = jnp.where(low, pltpu.roll(first, SLAB, 0), second)


def pick_pair(source, rows, slot_a, slot_b, none, first_half):
    def one(slot, half):
        there = slot != none
        safe = jnp.where(there, slot, 0)
        block = source[safe >> 1, rows, :]
        turned = pltpu.roll(block, BLOCK, 1)
        same = (safe & 1) == half
        return jnp.where(there, jnp.where(same, block, turned), 0.0)

    return jnp.where(first_half, one(slot_a, 0), one(slot_b, 1))


def class_kernel(table_ref, s0, s1, s2, s3, own_ref, to_right, to_left, chunks):
    for r, shard in enumerate((s0, s1, s2, s3)):
        chunks[2 * r] = shard[:, 0:128]
        chunks[2 * r + 1] = shard[:, 128:256]
    first_half = lax.broadcasted_iota(jnp.int32, (BLOCK, HALF), 1) < BLOCK
    for i in range(OWN):
        rows = slice(i * BLOCK, (i + 1) * BLOCK)
        for q in range(CLASS // 2):
            at = AT_SLOT + i * CLASS + 2 * q
            block = pick_pair(chunks, rows, table_ref[at], table_ref[at + 1], KNZ, first_half)
            own_ref[rows, q * 128 : (q + 1) * 128] = block
            if q > 0:
                to_right[rows, (q - 1) * 128 : q * 128] = block
            if q < 2:
                to_left[rows, q * 128 : (q + 1) * 128] = block


def split(x):
    high = x.astype(jnp.bfloat16)
    return high, (x - high.astype(jnp.float32)).astype(jnp.bfloat16)


def product(table_ref, shards, own_ref, from_left, from_right, right_high, right_low, finish):
    empty = jnp.zeros((ROWS, 128), jnp.bfloat16)
    for source, row, col in ((from_left, 0, 0), (own_ref, ROWS, 0), (from_right, 2 * ROWS, 128)):
        width = source.shape[1]
        high, low = split(source[...])
        right_high[row : row + ROWS, col : col + width] = high
        right_low[row : row + ROWS, col : col + width] = low
    for store in (right_high, right_low):
        store[0:ROWS, WIDTH:CLASS_COLS] = empty
        store[2 * ROWS : 3 * ROWS, 0:128] = empty
    dot = functools.partial(jnp.dot, preferred_element_type=jnp.float32)
    for i in range(OWN):
        rows = slice(i * BLOCK, (i + 1) * BLOCK)
        total = jnp.zeros((BLOCK, CLASS_COLS), jnp.float32)
        for r, shard in enumerate(shards):
            high, low = split(shard[rows, :])
            places = [
                pl.ds(pl.multiple_of(table_ref[AT_ROW + i * KNZ + 4 * r + k] * BLOCK, BLOCK), BLOCK)
                for k in range(KNZ // LAYERS)
            ]
            weight_high = jnp.concatenate([right_high[p, :] for p in places], axis=0)
            weight_low = jnp.concatenate([right_low[p, :] for p in places], axis=0)
            both = dot(jnp.concatenate([high, low], axis=0), weight_high)
            total = total + both[:BLOCK] + both[BLOCK:] + dot(high, weight_low)
        finish(i, rows, total)


def square_kernel(
    table_ref, s0, s1, s2, s3, own_ref, from_left, from_right, square_ref, to_right, to_left, o0, o1, o2, o3, right_high, right_low, chunks
):
    first_half = lax.broadcasted_iota(jnp.int32, (BLOCK, HALF), 1) < BLOCK
    outs = (o0, o1, o2, o3)

    def finish(i, rows, total):
        for q in range(CLASS // 2):
            at = AT_KEEP + i * CLASS + 2 * q
            keep = jnp.where(first_half, table_ref[at], table_ref[at + 1]) != 0
            block = jnp.where(keep, total[:, q * 128 : (q + 1) * 128], 0.0)
            chunks[q, rows, :] = block
            square_ref[rows, q * 128 : (q + 1) * 128] = block
            if q > 0:
                to_right[rows, (q - 1) * 128 : q * 128] = block
            if q < 2:
                to_left[rows, q * 128 : (q + 1) * 128] = block
        for c in range(JNZ // 2):
            at = AT_REL + i * JNZ + 2 * c
            block = pick_pair(chunks, rows, table_ref[at], table_ref[at + 1], -1, first_half)
            outs[c // 2][rows, (c % 2) * 128 : (c % 2 + 1) * 128] = block

    product(table_ref, (s0, s1, s2, s3), own_ref, from_left, from_right, right_high, right_low, finish)


def cubic_kernel(
    table_ref, s0, s1, s2, s3, own_ref, from_left, from_right, keep_ref, o0, o1, o2, o3, right_high, right_low, chunks
):
    first_half = lax.broadcasted_iota(jnp.int32, (BLOCK, HALF), 1) < BLOCK
    outs = (o0, o1, o2, o3)

    def finish(i, rows, total):
        for q in range(CLASS // 2):
            cols = slice(q * 128, (q + 1) * 128)
            chunks[q, rows, :] = 1.5 * keep_ref[rows, cols] - 0.5 * total[:, cols]
        for c in range(JNZ // 2):
            at = AT_REL + i * JNZ + 2 * c
            block = pick_pair(chunks, rows, table_ref[at], table_ref[at + 1], -1, first_half)
            outs[c // 2][rows, (c % 2) * 128 : (c % 2 + 1) * 128] = block

    product(table_ref, (s0, s1, s2, s3), own_ref, from_left, from_right, right_high, right_low, finish)


RIGHT = [
    pltpu.VMEM((NEAR * BLOCK, CLASS_COLS), jnp.bfloat16),
    pltpu.VMEM((NEAR * BLOCK, CLASS_COLS), jnp.bfloat16),
    pltpu.VMEM((CLASS // 2, ROWS, HALF), jnp.float32),
]


def shift(x, axis, by):
    count = lax.axis_size(axis)
    return lax.ppermute(x, axis, [(i, (i + by) % count) for i in range(count)])


def gather_slots(parts):
    first, second, third = (shift(parts[r], "narrow", r) for r in range(1, LAYERS))
    return parts[0] + first + second + third


def tables(block_cols, filter_cols, wide_index, layer):
    first_row = wide_index * OWN
    base = first_row - OWN

    def own(cols):
        mine = lax.dynamic_slice_in_dim(cols, first_row, OWN, 0)
        mine = (mine - base) & (NBR - 1)
        turned = lax.dynamic_slice_in_dim(jnp.concatenate([mine, mine], axis=1), layer * (KNZ // LAYERS), KNZ, 1)
        return mine, turned

    _, cols = own(block_cols)
    kept, kept_turned = own(filter_cols)
    places = layer + LAYERS * jnp.arange(CLASS, dtype=jnp.int32)
    slots = jnp.arange(KNZ, dtype=jnp.int32)
    slot = jnp.min(jnp.where(cols[:, None, :] == places[None, :, None], slots, KNZ), axis=2)
    keep = jnp.max((kept[:, None, :] == places[None, :, None]).astype(jnp.int32), axis=2)

    def source(filters):
        return jnp.where((filters - layer) & (LAYERS - 1) == 0, (filters - layer) >> 2, -1)

    return jnp.concatenate([part.reshape(-1) for part in (cols, slot, keep, source(kept), source(kept_turned))])


def local(restart, slab_slot, block_cols, filter_cols):
    wide_index = lax.axis_index("wide")
    layer = lax.axis_index("narrow")
    table = tables(block_cols, filter_cols, wide_index, layer)

    packed = pl.pallas_call(
        pack_kernel,
        out_shape=f32(N_WIDE, 9, 1, 128),
        in_specs=[SMEM, VMEM],
        out_specs=VMEM,
        compiler_params=PARAMS,
        cost_estimate=cost(0, 1 << 20),
        name="pack",
    )(slab_slot, restart)
    arrived = lax.all_to_all(packed, "wide", split_axis=0, concat_axis=0, tiled=True)
    position = arrived[:, 8, 0, 0].astype(jnp.int32)
    mine = pl.pallas_call(
        unpack_kernel,
        out_shape=f32(ROWS, WIDTH),
        in_specs=[SMEM, VMEM],
        out_specs=VMEM,
        scratch_shapes=[pltpu.VMEM((SLABS, 8, 128), jnp.float32)],
        compiler_params=PARAMS,
        cost_estimate=cost(0, 1 << 20),
        name="unpack",
    )(position, arrived)
    shards = (mine, shift(mine, "narrow", -1), shift(mine, "narrow", -2), shift(mine, "narrow", -3))

    half = f32(ROWS, WIDTH)
    whole = f32(ROWS, CLASS_COLS)
    own, to_right, to_left = pl.pallas_call(
        class_kernel,
        out_shape=(whole, half, half),
        in_specs=[SMEM] + [VMEM] * 4,
        out_specs=(VMEM,) * 3,
        scratch_shapes=[pltpu.VMEM((2 * LAYERS, ROWS, HALF), jnp.float32)],
        compiler_params=PARAMS,
        cost_estimate=cost(0, 4 << 20),
        name="columns_of_class",
    )(table, *shards)
    from_left = shift(to_right, "wide", 1)
    from_right = shift(to_left, "wide", -1)

    flops = 2 * 3 * ROWS * KNZ * BLOCK * CLASS_COLS
    square, to_right, to_left, *slots = pl.pallas_call(
        square_kernel,
        out_shape=(whole,) + (half,) * 6,
        in_specs=[SMEM] + [VMEM] * 7,
        out_specs=(VMEM,) * 7,
        scratch_shapes=RIGHT,
        compiler_params=PARAMS,
        cost_estimate=cost(flops, 8 << 20),
        name="square",
    )(table, *shards, own, from_left, from_right)
    from_left = shift(to_right, "wide", 1)
    from_right = shift(to_left, "wide", -1)

    squared = gather_slots(slots)
    parts = pl.pallas_call(
        cubic_kernel,
        out_shape=(half,) * 4,
        in_specs=[SMEM] + [VMEM] * 8,
        out_specs=(VMEM,) * 4,
        scratch_shapes=RIGHT,
        compiler_params=PARAMS,
        cost_estimate=cost(flops, 8 << 20),
        name="cubic",
    )(table, *shards, square, from_left, from_right, own)
    updated = gather_slots(parts)
    return (squared, updated)


def solution(mesh):
    placed = (P("wide", "narrow"), P("wide"), P(), P())
    return jax.shard_map(
        local,
        mesh=mesh,
        in_specs=placed,
        out_specs=(P("wide", "narrow"), P("wide", "narrow")),
        check_vma=False,
    )
```

```python
import functools

import jax
import jax.numpy as jnp
from jax import lax
from jax.experimental import pallas as pl
from jax.experimental.pallas import tpu as pltpu
from jax.sharding import PartitionSpec as P

BLOCK = 64
KNZ = 16
JNZ = 16
SLAB = 4
N_WIDE = 128
LAYERS = 4
OWN = 8
NBR = 1024
SLABS = 128
ROWS = OWN * BLOCK
WIDTH = 256
CLASS = 6
CLASS_COLS = CLASS * BLOCK
NEAR = 3 * OWN
HALF = 2 * BLOCK
KEPT = JNZ // LAYERS
MOST = OWN * KEPT
FIRST = 18
LATE = MOST - FIRST

AT_ROW = 0
AT_SLOT = AT_ROW + OWN * KNZ
AT_KEEP = AT_SLOT + OWN * CLASS
AT_SEND = AT_KEEP + OWN * CLASS
AT_PLACE = AT_SEND + LAYERS * OWN * KEPT
AT_LATE = AT_PLACE + OWN * KEPT

VMEM = pl.BlockSpec(memory_space=pltpu.VMEM)
SMEM = pl.BlockSpec(memory_space=pltpu.SMEM)
PARAMS = pltpu.CompilerParams(vmem_limit_bytes=24 * 1024 * 1024)


def cost(flops, bytes_accessed):
    return pl.CostEstimate(flops=flops, bytes_accessed=bytes_accessed, transcendentals=0)


def f32(*shape):
    return jax.ShapeDtypeStruct(shape, jnp.float32)


def pack_kernel(slot_ref, rows_ref, out_ref):
    low = lax.broadcasted_iota(jnp.int32, (8, 128), 0) < SLAB
    for pair in range(SLABS // 2):
        left = rows_ref[8 * pair : 8 * pair + 8, 0:128]
        right = rows_ref[8 * pair : 8 * pair + 8, 128:256]
        first = jnp.where(low, left, pltpu.roll(right, SLAB, 0))
        second = jnp.where(low, pltpu.roll(left, SLAB, 0), right)
        for which, tile in ((0, first), (1, second)):
            slot = slot_ref[2 * pair + which]
            target = slot >> 7
            out_ref[target, 0:8] = tile.reshape(8, 1, 128)
            out_ref[target, 8] = jnp.full((1, 128), (slot & 127).astype(jnp.float32))


def unpack_kernel(arrived_ref, rows_ref, tiles, places, *halves):
    for source in range(N_WIDE):
        tiles[8 * source : 8 * source + 8, :] = arrived_ref[source, 0:8].reshape(8, 128)
        places[source : source + 1, :] = arrived_ref[source, 8]
    order = lax.broadcasted_iota(jnp.int32, (SLABS, N_WIDE), 0).astype(jnp.float32)
    chosen = (jnp.transpose(places[...]) == order).astype(jnp.bfloat16)
    for row in range(8):
        rest = tiles[pl.ds(row, N_WIDE, stride=8), :]
        found = jnp.zeros((SLABS, 128), jnp.float32)
        for _ in range(3):
            part = rest.astype(jnp.bfloat16)
            rest = rest - part.astype(jnp.float32)
            found = found + jnp.dot(chosen, part, preferred_element_type=jnp.float32)
        half = row // SLAB
        halves[half][pl.ds(row % SLAB, SLABS, stride=SLAB), :] = found
    for half in range(2):
        rows_ref[:, half * 128 : (half + 1) * 128] = halves[half][...]


def pick(source, chunk, row, half, there, wanted, other=0.0):
    block = source[chunk, pl.ds(pl.multiple_of(row, BLOCK), BLOCK), :]
    return jnp.where(there, jnp.where(half == wanted, block, pltpu.roll(block, BLOCK, 1)), other)


def first_lanes():
    return lax.broadcasted_iota(jnp.int32, (BLOCK, HALF), 1) < BLOCK


def pack_blocks(table_ref, source, out_ref, at):
    first_half = first_lanes()

    def one(entry, wanted):
        there = entry >= 0
        place = entry & (OWN - 1)
        row = (jnp.maximum(entry, 0) >> 3) * BLOCK
        return pick(source, jnp.where(there, place >> 1, 0), row, place & 1, there, wanted)

    for pair in range(out_ref.shape[0] // BLOCK):
        block = jnp.where(first_half, one(table_ref[at + 2 * pair], 0), one(table_ref[at + 2 * pair + 1], 1))
        out_ref[pair * BLOCK : (pair + 1) * BLOCK, :] = block


def place_blocks(table_ref, source, out_ref, at, before=None):
    first_half = first_lanes()
    for i in range(OWN):
        rows = slice(i * BLOCK, (i + 1) * BLOCK)
        for c in range(KEPT // 2):
            cols = slice(c * HALF, (c + 1) * HALF)
            other = 0.0 if before is None else before[rows, cols]

            def one(entry, wanted):
                safe = jnp.maximum(entry, 0)
                return pick(source, 0, (safe >> 1) * BLOCK, safe & 1, entry >= 0, wanted, other)

            slot = at + i * KEPT + 2 * c
            out_ref[rows, cols] = jnp.where(first_half, one(table_ref[slot], 0), one(table_ref[slot + 1], 1))


def stack_blocks(parts, stacked):
    row = 0
    for part in parts:
        stacked[0, row : row + part.shape[0], :] = part[...]
        row += part.shape[0]


def place_kernel(table_ref, p0, p1, p2, p3, out_ref, stacked):
    stack_blocks((p0, p1, p2, p3), stacked)
    place_blocks(table_ref, stacked, out_ref, AT_PLACE)


def late_pack_kernel(table_ref, source_ref, o1, o2, o3, chunks):
    for q in range(CLASS // 2):
        chunks[q] = source_ref[:, q * HALF : (q + 1) * HALF]
    for r, out_ref in enumerate((o1, o2, o3)):
        pack_blocks(table_ref, chunks, out_ref, AT_SEND + (r + 1) * MOST + FIRST)


def late_place_kernel(table_ref, before_ref, p1, p2, p3, out_ref, stacked):
    stack_blocks((p1, p2, p3), stacked)
    place_blocks(table_ref, stacked, out_ref, AT_LATE, before_ref)


def class_kernel(table_ref, s0, s1, s2, s3, own_ref, to_right, to_left, chunks):
    for r, shard in enumerate((s0, s1, s2, s3)):
        chunks[2 * r] = shard[:, 0:128]
        chunks[2 * r + 1] = shard[:, 128:256]
    first_half = first_lanes()
    for i in range(OWN):
        rows = slice(i * BLOCK, (i + 1) * BLOCK)

        def one(slot, wanted):
            there = slot != KNZ
            safe = jnp.where(there, slot, 0)
            return pick(chunks, safe >> 1, i * BLOCK, safe & 1, there, wanted)

        for q in range(CLASS // 2):
            at = AT_SLOT + i * CLASS + 2 * q
            block = jnp.where(first_half, one(table_ref[at], 0), one(table_ref[at + 1], 1))
            own_ref[rows, q * 128 : (q + 1) * 128] = block
            if q > 0:
                to_right[rows, (q - 1) * 128 : q * 128] = block
            if q < 2:
                to_left[rows, q * 128 : (q + 1) * 128] = block


def split(x):
    high = x.astype(jnp.bfloat16)
    return high, (x - high.astype(jnp.float32)).astype(jnp.bfloat16)


def product(table_ref, shards, own_ref, from_left, from_right, right_high, right_low, finish):
    empty = jnp.zeros((ROWS, 128), jnp.bfloat16)
    for source, row, col in ((from_left, 0, 0), (own_ref, ROWS, 0), (from_right, 2 * ROWS, 128)):
        width = source.shape[1]
        high, low = split(source[...])
        right_high[row : row + ROWS, col : col + width] = high
        right_low[row : row + ROWS, col : col + width] = low
    for store in (right_high, right_low):
        store[0:ROWS, WIDTH:CLASS_COLS] = empty
        store[2 * ROWS : 3 * ROWS, 0:128] = empty
    dot = functools.partial(jnp.dot, preferred_element_type=jnp.float32)
    for i in range(OWN):
        rows = slice(i * BLOCK, (i + 1) * BLOCK)
        total = jnp.zeros((BLOCK, CLASS_COLS), jnp.float32)
        for r, shard in enumerate(shards):
            high, low = split(shard[rows, :])
            places = [
                pl.ds(pl.multiple_of(table_ref[AT_ROW + i * KNZ + 4 * r + k] * BLOCK, BLOCK), BLOCK)
                for k in range(KNZ // LAYERS)
            ]
            weight_high = jnp.concatenate([right_high[p, :] for p in places], axis=0)
            weight_low = jnp.concatenate([right_low[p, :] for p in places], axis=0)
            both = dot(jnp.concatenate([high, low], axis=0), weight_high)
            total = total + both[:BLOCK] + both[BLOCK:] + dot(high, weight_low)
        finish(i, rows, total)


def square_kernel(
    table_ref, s0, s1, s2, s3, own_ref, from_left, from_right, square_ref, to_right, to_left, o0, o1, o2, o3, right_high, right_low, chunks
):
    first_half = first_lanes()

    def finish(i, rows, total):
        for q in range(CLASS // 2):
            at = AT_KEEP + i * CLASS + 2 * q
            keep = jnp.where(first_half, table_ref[at], table_ref[at + 1]) != 0
            block = jnp.where(keep, total[:, q * 128 : (q + 1) * 128], 0.0)
            chunks[q, rows, :] = block
            square_ref[rows, q * 128 : (q + 1) * 128] = block
            if q > 0:
                to_right[rows, (q - 1) * 128 : q * 128] = block
            if q < 2:
                to_left[rows, q * 128 : (q + 1) * 128] = block

    product(table_ref, (s0, s1, s2, s3), own_ref, from_left, from_right, right_high, right_low, finish)
    for r, out_ref in enumerate((o0, o1, o2, o3)):
        pack_blocks(table_ref, chunks, out_ref, AT_SEND + r * MOST)


def cubic_kernel(
    table_ref, s0, s1, s2, s3, own_ref, from_left, from_right, keep_ref, step_ref, o0, o1, o2, o3, right_high, right_low, chunks
):

    def finish(i, rows, total):
        for q in range(CLASS // 2):
            cols = slice(q * 128, (q + 1) * 128)
            block = 1.5 * keep_ref[rows, cols] - 0.5 * total[:, cols]
            chunks[q, rows, :] = block
            step_ref[rows, cols] = block

    product(table_ref, (s0, s1, s2, s3), own_ref, from_left, from_right, right_high, right_low, finish)
    for r, out_ref in enumerate((o0, o1, o2, o3)):
        pack_blocks(table_ref, chunks, out_ref, AT_SEND + r * MOST)


RIGHT = [
    pltpu.VMEM((NEAR * BLOCK, CLASS_COLS), jnp.bfloat16),
    pltpu.VMEM((NEAR * BLOCK, CLASS_COLS), jnp.bfloat16),
    pltpu.VMEM((CLASS // 2, ROWS, HALF), jnp.float32),
]


def shift(x, axis, by):
    count = lax.axis_size(axis)
    return lax.ppermute(x, axis, [(i, (i + by) % count) for i in range(count)])


def call(kernel, name, outs, *operands, scratch=(), size=1 << 20, flops=0, scalars=1):
    single = not isinstance(outs, tuple)
    return pl.pallas_call(
        kernel,
        out_shape=outs,
        in_specs=[SMEM] * scalars + [VMEM] * (len(operands) - scalars),
        out_specs=VMEM if single else (VMEM,) * len(outs),
        scratch_shapes=list(scratch),
        compiler_params=PARAMS,
        cost_estimate=cost(flops, size),
        name=name,
    )(*operands)


def blocks(count):
    return f32(count // 2 * BLOCK, HALF)


def send_parts(parts):
    return tuple(shift(part, "narrow", r + 1) for r, part in enumerate(parts))


def place(table, own, parts):
    stacked = pltpu.VMEM((1, (MOST + 3 * FIRST) // 2 * BLOCK, HALF), jnp.float32)
    return call(place_kernel, "place_blocks", f32(ROWS, WIDTH), table, own, *parts, scratch=(stacked,))


def place_late(table, before, source):
    chunks = pltpu.VMEM((CLASS // 2, ROWS, HALF), jnp.float32)
    parts = call(late_pack_kernel, "late_blocks", (blocks(LATE),) * 3, table, source, scratch=(chunks,))
    stacked = pltpu.VMEM((1, 3 * LATE // 2 * BLOCK, HALF), jnp.float32)
    return call(late_place_kernel, "place_late_blocks", f32(ROWS, WIDTH), table, before, *send_parts(parts), scratch=(stacked,))


def any_late(filter_cols):
    ones = jnp.left_shift(1, 8 * (filter_cols & (LAYERS - 1)))
    counts = jnp.sum(ones.reshape(N_WIDE, OWN, LAYERS, KEPT), axis=(1, 3))
    layers = jnp.arange(LAYERS, dtype=jnp.int32)
    each = (counts[:, :, None] >> (8 * layers)) & 255
    return jnp.max(jnp.where(layers[:, None] == layers, 0, each)) > FIRST


def tables(block_cols, filter_cols, wide_index, layer):
    first_row = wide_index * OWN
    base = first_row - OWN

    def own(cols):
        mine = lax.dynamic_slice_in_dim(cols, first_row, OWN, 0)
        mine = (mine - base) & (NBR - 1)
        turned = lax.dynamic_slice_in_dim(jnp.concatenate([mine, mine], axis=1), layer * (KNZ // LAYERS), KNZ, 1)
        return mine, turned

    _, cols = own(block_cols)
    kept, kept_turned = own(filter_cols)
    places = layer + LAYERS * jnp.arange(CLASS, dtype=jnp.int32)
    slots = jnp.arange(KNZ, dtype=jnp.int32)
    slot = jnp.min(jnp.where(cols[:, None, :] == places[None, :, None], slots, KNZ), axis=2)
    keep = jnp.max((kept[:, None, :] == places[None, :, None]).astype(jnp.int32), axis=2)

    wanted = kept_turned.reshape(OWN, LAYERS, KEPT).transpose(1, 0, 2).reshape(LAYERS, MOST)
    here = (wanted & (LAYERS - 1)) == layer
    order = jnp.arange(MOST, dtype=jnp.int32)
    earlier = order[None, :] < order[:, None]
    rank = jnp.sum((here[:, None, :] & earlier).astype(jnp.int32), axis=2)
    code = (order >> 2) * OWN + ((wanted - layer) >> 2)
    chosen = here[:, None, :] & (rank[:, None, :] == order[None, :, None])
    send = jnp.max(jnp.where(chosen, code[:, None, :], -1), axis=2)
    group = wanted[0] & (LAYERS - 1)
    source = (layer - group) & (LAYERS - 1)
    place = jnp.sum(((group[None, :] == group[:, None]) & earlier).astype(jnp.int32), axis=1)
    mine = source == 0
    first = jnp.where(mine, place, MOST + FIRST * (source - 1) + place)
    late = jnp.logical_not(mine) & (place >= FIRST)
    first = jnp.where(late, -1, first)
    late = jnp.where(late, LATE * (source - 1) + place - FIRST, -1)
    return jnp.concatenate([part.reshape(-1) for part in (cols, slot, keep, send, first, late)])


def local(restart, slab_slot, block_cols, filter_cols):
    wide_index = lax.axis_index("wide")
    layer = lax.axis_index("narrow")
    table, late = lax.optimization_barrier((tables(block_cols, filter_cols, wide_index, layer), any_late(filter_cols)))

    packed = call(pack_kernel, "pack", f32(N_WIDE, 9, 1, 128), slab_slot, restart)
    arrived = lax.all_to_all(packed, "wide", split_axis=0, concat_axis=0, tiled=True)
    scratch = (pltpu.VMEM((8 * N_WIDE, 128), jnp.float32), pltpu.VMEM((N_WIDE, 128), jnp.float32)) + (pltpu.VMEM((ROWS, 128), jnp.float32),) * 2
    mine = call(unpack_kernel, "unpack", f32(ROWS, WIDTH), arrived, scratch=scratch, scalars=0)
    shards = (mine, shift(mine, "narrow", -1), shift(mine, "narrow", -2), shift(mine, "narrow", -3))

    half = f32(ROWS, WIDTH)
    whole = f32(ROWS, CLASS_COLS)
    sent = (blocks(MOST), blocks(FIRST), blocks(FIRST), blocks(FIRST))
    flops = 2 * 3 * ROWS * KNZ * BLOCK * CLASS_COLS
    chunks = pltpu.VMEM((2 * LAYERS, ROWS, HALF), jnp.float32)
    own, to_right, to_left = call(class_kernel, "columns_of_class", (whole, half, half), table, *shards, scratch=(chunks,), size=4 << 20)
    from_left = shift(to_right, "wide", 1)
    from_right = shift(to_left, "wide", -1)

    square, to_right, to_left, *parts = call(
        square_kernel, "square", (whole, half, half) + sent, table, *shards, own, from_left, from_right,
        scratch=RIGHT, size=8 << 20, flops=flops,
    )
    from_left = shift(to_right, "wide", 1)
    from_right = shift(to_left, "wide", -1)
    squared = place(table, parts[0], send_parts(parts[1:]))

    step, *parts = call(
        cubic_kernel, "cubic", (whole,) + sent, table, *shards, square, from_left, from_right, own,
        scratch=RIGHT, size=8 << 20, flops=flops,
    )
    updated = place(table, parts[0], send_parts(parts[1:]))

    def with_late(state):
        _, squared, updated = state
        return jnp.zeros((), bool), place_late(table, squared, square), place_late(table, updated, step)

    return lax.while_loop(lambda state: state[0], with_late, (late, squared, updated))[1:]


def solution(mesh):
    placed = (P("wide", "narrow"), P("wide"), P(), P())
    return jax.shard_map(
        local,
        mesh=mesh,
        in_specs=placed,
        out_specs=(P("wide", "narrow"), P("wide", "narrow")),
        check_vma=False,
    )
```

```python
import functools

import jax
import jax.numpy as jnp
from jax import lax
from jax.experimental import pallas as pl
from jax.experimental.pallas import tpu as pltpu
from jax.sharding import PartitionSpec as P

BLOCK = 64
KNZ = 16
JNZ = 16
SLAB = 4
N_WIDE = 128
LAYERS = 4
OWN = 8
NBR = 1024
SLABS = 128
ROWS = OWN * BLOCK
WIDTH = 256
CLASS = 6
CLASS_COLS = CLASS * BLOCK
NEAR = 3 * OWN
HALF = 2 * BLOCK
KEPT = JNZ // LAYERS
MOST = OWN * KEPT
FIRST = 18
LATE = MOST - FIRST

AT_ROW = 0
AT_SLOT = AT_ROW + OWN * KNZ
AT_KEEP = AT_SLOT + OWN * CLASS
AT_SEND = AT_KEEP + OWN * CLASS
AT_PLACE = AT_SEND + LAYERS * OWN * KEPT
AT_LATE = AT_PLACE + OWN * KEPT
AT_ODD = AT_LATE + OWN * KEPT

VMEM = pl.BlockSpec(memory_space=pltpu.VMEM)
SMEM = pl.BlockSpec(memory_space=pltpu.SMEM)
PARAMS = pltpu.CompilerParams(vmem_limit_bytes=24 * 1024 * 1024)


def cost(flops, bytes_accessed):
    return pl.CostEstimate(flops=flops, bytes_accessed=bytes_accessed, transcendentals=0)


def f32(*shape):
    return jax.ShapeDtypeStruct(shape, jnp.float32)


def pack_kernel(slot_ref, rows_ref, out_ref):
    low = lax.broadcasted_iota(jnp.int32, (8, 128), 0) < SLAB
    for pair in range(SLABS // 2):
        left = rows_ref[8 * pair : 8 * pair + 8, 0:128]
        right = rows_ref[8 * pair : 8 * pair + 8, 128:256]
        first = jnp.where(low, left, pltpu.roll(right, SLAB, 0))
        second = jnp.where(low, pltpu.roll(left, SLAB, 0), right)
        for which, tile in ((0, first), (1, second)):
            slot = slot_ref[2 * pair + which]
            target = slot >> 7
            out_ref[target, 0:8] = tile.reshape(8, 1, 128)
            out_ref[target, 8] = jnp.full((1, 128), (slot & 127).astype(jnp.float32))


def unpack_kernel(arrived_ref, rows_ref, tiles, places, *halves):
    for source in range(N_WIDE):
        tiles[8 * source : 8 * source + 8, :] = arrived_ref[source, 0:8].reshape(8, 128)
        places[source : source + 1, :] = arrived_ref[source, 8]
    order = lax.broadcasted_iota(jnp.int32, (SLABS, N_WIDE), 0).astype(jnp.float32)
    chosen = (jnp.transpose(places[...]) == order).astype(jnp.bfloat16)
    for row in range(8):
        rest = tiles[pl.ds(row, N_WIDE, stride=8), :]
        found = jnp.zeros((SLABS, 128), jnp.float32)
        for _ in range(3):
            part = rest.astype(jnp.bfloat16)
            rest = rest - part.astype(jnp.float32)
            found = found + jnp.dot(chosen, part, preferred_element_type=jnp.float32)
        half = row // SLAB
        halves[half][pl.ds(row % SLAB, SLABS, stride=SLAB), :] = found
    for half in range(2):
        rows_ref[:, half * 128 : (half + 1) * 128] = halves[half][...]


def pick(source, chunk, row, half, there, wanted, other=0.0):
    block = source[chunk, pl.ds(pl.multiple_of(row, BLOCK), BLOCK), :]
    return jnp.where(there, jnp.where(half == wanted, block, pltpu.roll(block, BLOCK, 1)), other)


def first_lanes():
    return lax.broadcasted_iota(jnp.int32, (BLOCK, HALF), 1) < BLOCK


def pack_blocks(table_ref, source, out_ref, at):
    first_half = first_lanes()

    def one(entry, wanted):
        there = entry >= 0
        place = entry & (OWN - 1)
        row = (jnp.maximum(entry, 0) >> 3) * BLOCK
        return pick(source, jnp.where(there, place >> 1, 0), row, place & 1, there, wanted)

    for pair in range(out_ref.shape[0] // BLOCK):
        block = jnp.where(first_half, one(table_ref[at + 2 * pair], 0), one(table_ref[at + 2 * pair + 1], 1))
        out_ref[pair * BLOCK : (pair + 1) * BLOCK, :] = block


def place_blocks(table_ref, source, out_ref, at, before=None):
    first_half = first_lanes()
    for i in range(OWN):
        rows = slice(i * BLOCK, (i + 1) * BLOCK)
        for c in range(KEPT // 2):
            cols = slice(c * HALF, (c + 1) * HALF)
            other = 0.0 if before is None else before[rows, cols]

            def one(entry, wanted):
                safe = jnp.maximum(entry, 0)
                return pick(source, 0, (safe >> 1) * BLOCK, safe & 1, entry >= 0, wanted, other)

            slot = at + i * KEPT + 2 * c
            out_ref[rows, cols] = jnp.where(first_half, one(table_ref[slot], 0), one(table_ref[slot + 1], 1))


def stack_blocks(parts, stacked):
    row = 0
    for part in parts:
        stacked[0, row : row + part.shape[0], :] = part[...]
        row += part.shape[0]


def place_kernel(table_ref, p0, p1, p2, p3, out_ref, stacked):
    stack_blocks((p0, p1, p2, p3), stacked)
    place_blocks(table_ref, stacked, out_ref, AT_PLACE)


def late_pack_kernel(table_ref, source_ref, o1, o2, o3, chunks):
    for q in range(CLASS // 2):
        chunks[q] = source_ref[:, q * HALF : (q + 1) * HALF]
    for r, out_ref in enumerate((o1, o2, o3)):
        pack_blocks(table_ref, chunks, out_ref, AT_SEND + (r + 1) * MOST + FIRST)


def late_place_kernel(table_ref, before_ref, p1, p2, p3, out_ref, stacked):
    stack_blocks((p1, p2, p3), stacked)
    place_blocks(table_ref, stacked, out_ref, AT_LATE, before_ref)


def write_halos(table_ref, source, cross_ref, inner_ref):
    odd = table_ref[AT_ODD]
    for q in range(2):
        cols = slice(q * HALF, (q + 1) * HALF)
        cross_ref[:, cols] = source[odd + q]
        inner_ref[:, cols] = source[1 - odd + q]


def class_kernel(table_ref, s0, s1, s2, s3, own_ref, cross_ref, inner_ref, chunks, mine):
    for r, shard in enumerate((s0, s1, s2, s3)):
        chunks[2 * r] = shard[:, 0:128]
        chunks[2 * r + 1] = shard[:, 128:256]
    first_half = first_lanes()
    for i in range(OWN):
        rows = slice(i * BLOCK, (i + 1) * BLOCK)

        def one(slot, wanted):
            there = slot != KNZ
            safe = jnp.where(there, slot, 0)
            return pick(chunks, safe >> 1, i * BLOCK, safe & 1, there, wanted)

        for q in range(CLASS // 2):
            at = AT_SLOT + i * CLASS + 2 * q
            block = jnp.where(first_half, one(table_ref[at], 0), one(table_ref[at + 1], 1))
            own_ref[rows, q * 128 : (q + 1) * 128] = block
            mine[q, rows, :] = block
    write_halos(table_ref, mine, cross_ref, inner_ref)


def split(x):
    high = x.astype(jnp.bfloat16)
    return high, (x - high.astype(jnp.float32)).astype(jnp.bfloat16)


def product(table_ref, shards, own_ref, cross, inner, right_high, right_low, finish):
    empty = jnp.zeros((ROWS, 128), jnp.bfloat16)
    odd = table_ref[AT_ODD]
    for source, side in ((cross, odd), (own_ref, None), (inner, 1 - odd)):
        for q in range(source.shape[1] // HALF):
            high, low = split(source[:, q * HALF : (q + 1) * HALF])
            if side is None:
                place = (slice(ROWS, 2 * ROWS), slice(q * HALF, (q + 1) * HALF))
            else:
                place = (
                    pl.ds(pl.multiple_of(side * 2 * ROWS, 2 * ROWS), ROWS),
                    pl.ds(pl.multiple_of((side + q) * HALF, HALF), HALF),
                )
            right_high[place] = high
            right_low[place] = low
    for store in (right_high, right_low):
        store[0:ROWS, WIDTH:CLASS_COLS] = empty
        store[2 * ROWS : 3 * ROWS, 0:128] = empty
    dot = functools.partial(jnp.dot, preferred_element_type=jnp.float32)
    for i in range(OWN):
        rows = slice(i * BLOCK, (i + 1) * BLOCK)
        total = jnp.zeros((BLOCK, CLASS_COLS), jnp.float32)
        for r, shard in enumerate(shards):
            high, low = split(shard[rows, :])
            places = [
                pl.ds(pl.multiple_of(table_ref[AT_ROW + i * KNZ + 4 * r + k] * BLOCK, BLOCK), BLOCK)
                for k in range(KNZ // LAYERS)
            ]
            weight_high = jnp.concatenate([right_high[p, :] for p in places], axis=0)
            weight_low = jnp.concatenate([right_low[p, :] for p in places], axis=0)
            both = dot(jnp.concatenate([high, low], axis=0), weight_high)
            total = total + both[:BLOCK] + both[BLOCK:] + dot(high, weight_low)
        finish(i, rows, total)


def square_kernel(
    table_ref, s0, s1, s2, s3, own_ref, cross, inner, square_ref, to_cross, to_inner, o0, o1, o2, o3, right_high, right_low, chunks
):
    first_half = first_lanes()

    def finish(i, rows, total):
        for q in range(CLASS // 2):
            at = AT_KEEP + i * CLASS + 2 * q
            keep = jnp.where(first_half, table_ref[at], table_ref[at + 1]) != 0
            block = jnp.where(keep, total[:, q * 128 : (q + 1) * 128], 0.0)
            chunks[q, rows, :] = block
            square_ref[rows, q * 128 : (q + 1) * 128] = block

    product(table_ref, (s0, s1, s2, s3), own_ref, cross, inner, right_high, right_low, finish)
    write_halos(table_ref, chunks, to_cross, to_inner)
    for r, out_ref in enumerate((o0, o1, o2, o3)):
        pack_blocks(table_ref, chunks, out_ref, AT_SEND + r * MOST)


def cubic_kernel(
    table_ref, s0, s1, s2, s3, own_ref, cross, inner, keep_ref, step_ref, o0, o1, o2, o3, right_high, right_low, chunks
):

    def finish(i, rows, total):
        for q in range(CLASS // 2):
            cols = slice(q * 128, (q + 1) * 128)
            block = 1.5 * keep_ref[rows, cols] - 0.5 * total[:, cols]
            chunks[q, rows, :] = block
            step_ref[rows, cols] = block

    product(table_ref, (s0, s1, s2, s3), own_ref, cross, inner, right_high, right_low, finish)
    for r, out_ref in enumerate((o0, o1, o2, o3)):
        pack_blocks(table_ref, chunks, out_ref, AT_SEND + r * MOST)


RIGHT = [
    pltpu.VMEM((NEAR * BLOCK, CLASS_COLS), jnp.bfloat16),
    pltpu.VMEM((NEAR * BLOCK, CLASS_COLS), jnp.bfloat16),
    pltpu.VMEM((CLASS // 2, ROWS, HALF), jnp.float32),
]


def shift(x, axis, by):
    count = lax.axis_size(axis)
    return lax.ppermute(x, axis, [(i, (i + by) % count) for i in range(count)])


def call(kernel, name, outs, *operands, scratch=(), size=1 << 20, flops=0, scalars=1):
    single = not isinstance(outs, tuple)
    return pl.pallas_call(
        kernel,
        out_shape=outs,
        in_specs=[SMEM] * scalars + [VMEM] * (len(operands) - scalars),
        out_specs=VMEM if single else (VMEM,) * len(outs),
        scratch_shapes=list(scratch),
        compiler_params=PARAMS,
        cost_estimate=cost(flops, size),
        name=name,
    )(*operands)


def blocks(count):
    return f32(count // 2 * BLOCK, HALF)


def send_parts(parts):
    return tuple(shift(part, "narrow", r + 1) for r, part in enumerate(parts))


def place(table, own, parts):
    stacked = pltpu.VMEM((1, (MOST + 3 * FIRST) // 2 * BLOCK, HALF), jnp.float32)
    return call(place_kernel, "place_blocks", f32(ROWS, WIDTH), table, own, *parts, scratch=(stacked,))


def place_late(table, before, source):
    chunks = pltpu.VMEM((CLASS // 2, ROWS, HALF), jnp.float32)
    parts = call(late_pack_kernel, "late_blocks", (blocks(LATE),) * 3, table, source, scratch=(chunks,))
    stacked = pltpu.VMEM((1, 3 * LATE // 2 * BLOCK, HALF), jnp.float32)
    return call(late_place_kernel, "place_late_blocks", f32(ROWS, WIDTH), table, before, *send_parts(parts), scratch=(stacked,))


def any_late(filter_cols):
    ones = jnp.left_shift(1, 8 * (filter_cols & (LAYERS - 1)))
    counts = jnp.sum(ones.reshape(N_WIDE, OWN, LAYERS, KEPT), axis=(1, 3))
    layers = jnp.arange(LAYERS, dtype=jnp.int32)
    each = (counts[:, :, None] >> (8 * layers)) & 255
    return jnp.max(jnp.where(layers[:, None] == layers, 0, each)) > FIRST


def halos(cross, inner):
    count = lax.axis_size("wide")
    over = [(i, (i + 1) % count if i % 2 else (i - 1) % count) for i in range(count)]
    return lax.ppermute(cross, "wide", over), lax.ppermute(inner, "wide", [(i, i ^ 1) for i in range(count)])


def tables(block_cols, filter_cols, wide_index, layer):
    first_row = wide_index * OWN
    base = first_row - OWN

    def own(cols):
        mine = lax.dynamic_slice_in_dim(cols, first_row, OWN, 0)
        mine = (mine - base) & (NBR - 1)
        turned = lax.dynamic_slice_in_dim(jnp.concatenate([mine, mine], axis=1), layer * (KNZ // LAYERS), KNZ, 1)
        return mine, turned

    _, cols = own(block_cols)
    kept, kept_turned = own(filter_cols)
    places = layer + LAYERS * jnp.arange(CLASS, dtype=jnp.int32)
    slots = jnp.arange(KNZ, dtype=jnp.int32)
    slot = jnp.min(jnp.where(cols[:, None, :] == places[None, :, None], slots, KNZ), axis=2)
    keep = jnp.max((kept[:, None, :] == places[None, :, None]).astype(jnp.int32), axis=2)

    wanted = kept_turned.reshape(OWN, LAYERS, KEPT).transpose(1, 0, 2).reshape(LAYERS, MOST)
    here = (wanted & (LAYERS - 1)) == layer
    order = jnp.arange(MOST, dtype=jnp.int32)
    earlier = order[None, :] < order[:, None]
    rank = jnp.sum((here[:, None, :] & earlier).astype(jnp.int32), axis=2)
    code = (order >> 2) * OWN + ((wanted - layer) >> 2)
    chosen = here[:, None, :] & (rank[:, None, :] == order[None, :, None])
    send = jnp.max(jnp.where(chosen, code[:, None, :], -1), axis=2)
    group = wanted[0] & (LAYERS - 1)
    source = (layer - group) & (LAYERS - 1)
    place = jnp.sum(((group[None, :] == group[:, None]) & earlier).astype(jnp.int32), axis=1)
    mine = source == 0
    first = jnp.where(mine, place, MOST + FIRST * (source - 1) + place)
    late = jnp.logical_not(mine) & (place >= FIRST)
    first = jnp.where(late, -1, first)
    late = jnp.where(late, LATE * (source - 1) + place - FIRST, -1)
    return jnp.concatenate([jnp.reshape(part, -1) for part in (cols, slot, keep, send, first, late, wide_index & 1)])


def local(restart, slab_slot, block_cols, filter_cols):
    wide_index = lax.axis_index("wide")
    layer = lax.axis_index("narrow")
    table, late = lax.optimization_barrier((tables(block_cols, filter_cols, wide_index, layer), any_late(filter_cols)))

    packed = call(pack_kernel, "pack", f32(N_WIDE, 9, 1, 128), slab_slot, restart)
    arrived = lax.all_to_all(packed, "wide", split_axis=0, concat_axis=0, tiled=True)
    scratch = (pltpu.VMEM((8 * N_WIDE, 128), jnp.float32), pltpu.VMEM((N_WIDE, 128), jnp.float32)) + (pltpu.VMEM((ROWS, 128), jnp.float32),) * 2
    mine = call(unpack_kernel, "unpack", f32(ROWS, WIDTH), arrived, scratch=scratch, scalars=0)
    shards = (mine, shift(mine, "narrow", -1), shift(mine, "narrow", -2), shift(mine, "narrow", -3))

    half = f32(ROWS, WIDTH)
    whole = f32(ROWS, CLASS_COLS)
    sent = (blocks(MOST), blocks(FIRST), blocks(FIRST), blocks(FIRST))
    flops = 2 * 3 * ROWS * KNZ * BLOCK * CLASS_COLS
    chunks = pltpu.VMEM((2 * LAYERS, ROWS, HALF), jnp.float32)
    own, cross, inner = call(
        class_kernel, "columns_of_class", (whole, half, half), table, *shards, scratch=(chunks, RIGHT[2]), size=4 << 20
    )
    cross, inner = halos(cross, inner)

    square, cross_next, inner_next, *parts = call(
        square_kernel, "square", (whole, half, half) + sent, table, *shards, own, cross, inner,
        scratch=RIGHT, size=8 << 20, flops=flops,
    )
    cross, inner = halos(cross_next, inner_next)
    squared = place(table, parts[0], send_parts(parts[1:]))

    step, *parts = call(
        cubic_kernel, "cubic", (whole,) + sent, table, *shards, square, cross, inner, own,
        scratch=RIGHT, size=8 << 20, flops=flops,
    )
    updated = place(table, parts[0], send_parts(parts[1:]))

    def with_late(state):
        _, squared, updated = state
        return jnp.zeros((), bool), place_late(table, squared, square), place_late(table, updated, step)

    return lax.while_loop(lambda state: state[0], with_late, (late, squared, updated))[1:]


def solution(mesh):
    placed = (P("wide", "narrow"), P("wide"), P(), P())
    return jax.shard_map(
        local,
        mesh=mesh,
        in_specs=placed,
        out_specs=(P("wide", "narrow"), P("wide", "narrow")),
        check_vma=False,
    )
```

```python
import functools

import jax
import jax.numpy as jnp
from jax import lax
from jax.experimental import pallas as pl
from jax.experimental.pallas import tpu as pltpu
from jax.sharding import PartitionSpec as P

BLOCK = 64
KNZ = 16
JNZ = 16
SLAB = 4
N_WIDE = 128
LAYERS = 4
OWN = 8
NBR = 1024
SLABS = 128
ROWS = OWN * BLOCK
WIDTH = 256
CLASS = 6
CLASS_COLS = CLASS * BLOCK
NEAR = 3 * OWN
HALF = 2 * BLOCK
KEPT = JNZ // LAYERS
MOST = OWN * KEPT
FIRST = 16
LATE = MOST - FIRST

AT_ROW = 0
AT_SLOT = AT_ROW + OWN * KNZ
AT_KEEP = AT_SLOT + OWN * CLASS
AT_SEND = AT_KEEP + OWN * CLASS
AT_PLACE = AT_SEND + LAYERS * OWN * KEPT
AT_LATE = AT_PLACE + OWN * KEPT
AT_ODD = AT_LATE + OWN * KEPT

VMEM = pl.BlockSpec(memory_space=pltpu.VMEM)
SMEM = pl.BlockSpec(memory_space=pltpu.SMEM)
PARAMS = pltpu.CompilerParams(vmem_limit_bytes=24 * 1024 * 1024)


def cost(flops, bytes_accessed):
    return pl.CostEstimate(flops=flops, bytes_accessed=bytes_accessed, transcendentals=0)


def f32(*shape):
    return jax.ShapeDtypeStruct(shape, jnp.float32)


def pack_kernel(slot_ref, rows_ref, out_ref):
    low = lax.broadcasted_iota(jnp.int32, (8, 128), 0) < SLAB
    for pair in range(SLABS // 2):
        left = rows_ref[8 * pair : 8 * pair + 8, 0:128]
        right = rows_ref[8 * pair : 8 * pair + 8, 128:256]
        first = jnp.where(low, left, pltpu.roll(right, SLAB, 0))
        second = jnp.where(low, pltpu.roll(left, SLAB, 0), right)
        for which, tile in ((0, first), (1, second)):
            slot = slot_ref[2 * pair + which]
            target = slot >> 7
            out_ref[target, 0:8] = tile.reshape(8, 1, 128)
            out_ref[target, 8] = jnp.full((1, 128), (slot & 127).astype(jnp.float32))


def unpack_kernel(arrived_ref, rows_ref, tiles, places, *halves):
    for source in range(N_WIDE):
        tiles[8 * source : 8 * source + 8, :] = arrived_ref[source, 0:8].reshape(8, 128)
        places[source : source + 1, :] = arrived_ref[source, 8]
    order = lax.broadcasted_iota(jnp.int32, (SLABS, N_WIDE), 0).astype(jnp.float32)
    chosen = (jnp.transpose(places[...]) == order).astype(jnp.bfloat16)
    for row in range(8):
        rest = tiles[pl.ds(row, N_WIDE, stride=8), :]
        found = jnp.zeros((SLABS, 128), jnp.float32)
        for _ in range(3):
            part = rest.astype(jnp.bfloat16)
            rest = rest - part.astype(jnp.float32)
            found = found + jnp.dot(chosen, part, preferred_element_type=jnp.float32)
        half = row // SLAB
        halves[half][pl.ds(row % SLAB, SLABS, stride=SLAB), :] = found
    for half in range(2):
        rows_ref[:, half * 128 : (half + 1) * 128] = halves[half][...]


def pick(source, chunk, row, half, there, wanted, other=0.0):
    block = source[chunk, pl.ds(pl.multiple_of(row, BLOCK), BLOCK), :]
    return jnp.where(there, jnp.where(half == wanted, block, pltpu.roll(block, BLOCK, 1)), other)


def first_lanes():
    return lax.broadcasted_iota(jnp.int32, (BLOCK, HALF), 1) < BLOCK


def pack_blocks(table_ref, source, out_ref, at):
    first_half = first_lanes()

    def one(entry, wanted):
        there = entry >= 0
        place = entry & (OWN - 1)
        row = (jnp.maximum(entry, 0) >> 3) * BLOCK
        return pick(source, jnp.where(there, place >> 1, 0), row, place & 1, there, wanted)

    for pair in range(out_ref.shape[0] // BLOCK):
        block = jnp.where(first_half, one(table_ref[at + 2 * pair], 0), one(table_ref[at + 2 * pair + 1], 1))
        out_ref[pair * BLOCK : (pair + 1) * BLOCK, :] = block


def place_blocks(table_ref, source, out_ref, at, before=None):
    first_half = first_lanes()
    for i in range(OWN):
        rows = slice(i * BLOCK, (i + 1) * BLOCK)
        for c in range(KEPT // 2):
            cols = slice(c * HALF, (c + 1) * HALF)
            other = 0.0 if before is None else before[rows, cols]

            def one(entry, wanted):
                safe = jnp.maximum(entry, 0)
                return pick(source, 0, (safe >> 1) * BLOCK, safe & 1, entry >= 0, wanted, other)

            slot = at + i * KEPT + 2 * c
            out_ref[rows, cols] = jnp.where(first_half, one(table_ref[slot], 0), one(table_ref[slot + 1], 1))


def stack_blocks(parts, stacked):
    row = 0
    for part in parts:
        stacked[0, row : row + part.shape[0], :] = part[...]
        row += part.shape[0]


def place_kernel(table_ref, p0, p1, p2, p3, out_ref, stacked):
    stack_blocks((p0, p1, p2, p3), stacked)
    place_blocks(table_ref, stacked, out_ref, AT_PLACE)


def late_pack_kernel(table_ref, source_ref, o1, o2, o3, chunks):
    for q in range(CLASS // 2):
        chunks[q] = source_ref[:, q * HALF : (q + 1) * HALF]
    for r, out_ref in enumerate((o1, o2, o3)):
        pack_blocks(table_ref, chunks, out_ref, AT_SEND + (r + 1) * MOST + FIRST)


def late_place_kernel(table_ref, before_ref, p1, p2, p3, out_ref, stacked):
    stack_blocks((p1, p2, p3), stacked)
    place_blocks(table_ref, stacked, out_ref, AT_LATE, before_ref)


def write_halos(table_ref, source, cross_ref, inner_ref):
    odd = table_ref[AT_ODD]
    for q in range(2):
        cols = slice(q * HALF, (q + 1) * HALF)
        cross_ref[:, cols] = source[odd + q]
        inner_ref[:, cols] = source[1 - odd + q]


def class_kernel(table_ref, s0, s1, s2, s3, own_ref, cross_ref, inner_ref, chunks, mine):
    for r, shard in enumerate((s0, s1, s2, s3)):
        chunks[2 * r] = shard[:, 0:128]
        chunks[2 * r + 1] = shard[:, 128:256]
    first_half = first_lanes()
    for i in range(OWN):
        rows = slice(i * BLOCK, (i + 1) * BLOCK)

        def one(slot, wanted):
            there = slot != KNZ
            safe = jnp.where(there, slot, 0)
            return pick(chunks, safe >> 1, i * BLOCK, safe & 1, there, wanted)

        for q in range(CLASS // 2):
            at = AT_SLOT + i * CLASS + 2 * q
            block = jnp.where(first_half, one(table_ref[at], 0), one(table_ref[at + 1], 1))
            own_ref[rows, q * 128 : (q + 1) * 128] = block
            mine[q, rows, :] = block
    write_halos(table_ref, mine, cross_ref, inner_ref)


def split(x):
    high = x.astype(jnp.bfloat16)
    return high, (x - high.astype(jnp.float32)).astype(jnp.bfloat16)


def product(table_ref, shards, own_ref, cross, inner, right_high, right_low, finish):
    empty = jnp.zeros((ROWS, 128), jnp.bfloat16)
    odd = table_ref[AT_ODD]
    for source, side in ((cross, odd), (own_ref, None), (inner, 1 - odd)):
        for q in range(source.shape[1] // HALF):
            high, low = split(source[:, q * HALF : (q + 1) * HALF])
            if side is None:
                place = (slice(ROWS, 2 * ROWS), slice(q * HALF, (q + 1) * HALF))
            else:
                place = (
                    pl.ds(pl.multiple_of(side * 2 * ROWS, 2 * ROWS), ROWS),
                    pl.ds(pl.multiple_of((side + q) * HALF, HALF), HALF),
                )
            right_high[place] = high
            right_low[place] = low
    for store in (right_high, right_low):
        store[0:ROWS, WIDTH:CLASS_COLS] = empty
        store[2 * ROWS : 3 * ROWS, 0:128] = empty
    dot = functools.partial(jnp.dot, preferred_element_type=jnp.float32)
    for i in range(OWN):
        rows = slice(i * BLOCK, (i + 1) * BLOCK)
        total = jnp.zeros((BLOCK, CLASS_COLS), jnp.float32)
        for r, shard in enumerate(shards):
            high, low = split(shard[rows, :])
            places = [
                pl.ds(pl.multiple_of(table_ref[AT_ROW + i * KNZ + 4 * r + k] * BLOCK, BLOCK), BLOCK)
                for k in range(KNZ // LAYERS)
            ]
            weight_high = jnp.concatenate([right_high[p, :] for p in places], axis=0)
            weight_low = jnp.concatenate([right_low[p, :] for p in places], axis=0)
            both = dot(jnp.concatenate([high, low], axis=0), weight_high)
            total = total + both[:BLOCK] + both[BLOCK:] + dot(high, weight_low)
        finish(i, rows, total)


def square_kernel(
    table_ref, s0, s1, s2, s3, own_ref, cross, inner, square_ref, to_cross, to_inner, o0, o1, o2, o3, right_high, right_low, chunks
):
    first_half = first_lanes()

    def finish(i, rows, total):
        for q in range(CLASS // 2):
            at = AT_KEEP + i * CLASS + 2 * q
            keep = jnp.where(first_half, table_ref[at], table_ref[at + 1]) != 0
            block = jnp.where(keep, total[:, q * 128 : (q + 1) * 128], 0.0)
            chunks[q, rows, :] = block
            square_ref[rows, q * 128 : (q + 1) * 128] = block

    product(table_ref, (s0, s1, s2, s3), own_ref, cross, inner, right_high, right_low, finish)
    write_halos(table_ref, chunks, to_cross, to_inner)
    for r, out_ref in enumerate((o0, o1, o2, o3)):
        pack_blocks(table_ref, chunks, out_ref, AT_SEND + r * MOST)


def cubic_kernel(
    table_ref, s0, s1, s2, s3, own_ref, cross, inner, keep_ref, step_ref, o0, o1, o2, o3, right_high, right_low, chunks
):

    def finish(i, rows, total):
        for q in range(CLASS // 2):
            cols = slice(q * 128, (q + 1) * 128)
            block = 1.5 * keep_ref[rows, cols] - 0.5 * total[:, cols]
            chunks[q, rows, :] = block
            step_ref[rows, cols] = block

    product(table_ref, (s0, s1, s2, s3), own_ref, cross, inner, right_high, right_low, finish)
    for r, out_ref in enumerate((o0, o1, o2, o3)):
        pack_blocks(table_ref, chunks, out_ref, AT_SEND + r * MOST)


RIGHT = [
    pltpu.VMEM((NEAR * BLOCK, CLASS_COLS), jnp.bfloat16),
    pltpu.VMEM((NEAR * BLOCK, CLASS_COLS), jnp.bfloat16),
    pltpu.VMEM((CLASS // 2, ROWS, HALF), jnp.float32),
]


def shift(x, axis, by):
    count = lax.axis_size(axis)
    return lax.ppermute(x, axis, [(i, (i + by) % count) for i in range(count)])


def call(kernel, name, outs, *operands, scratch=(), size=1 << 20, flops=0, scalars=1):
    single = not isinstance(outs, tuple)
    return pl.pallas_call(
        kernel,
        out_shape=outs,
        in_specs=[SMEM] * scalars + [VMEM] * (len(operands) - scalars),
        out_specs=VMEM if single else (VMEM,) * len(outs),
        scratch_shapes=list(scratch),
        compiler_params=PARAMS,
        cost_estimate=cost(flops, size),
        name=name,
    )(*operands)


def blocks(count):
    return f32(count // 2 * BLOCK, HALF)


def send_parts(parts):
    return tuple(shift(part, "narrow", r + 1) for r, part in enumerate(parts))


def place(table, own, parts):
    stacked = pltpu.VMEM((1, (MOST + 3 * FIRST) // 2 * BLOCK, HALF), jnp.float32)
    return call(place_kernel, "place_blocks", f32(ROWS, WIDTH), table, own, *parts, scratch=(stacked,))


def place_late(table, before, source):
    chunks = pltpu.VMEM((CLASS // 2, ROWS, HALF), jnp.float32)
    parts = call(late_pack_kernel, "late_blocks", (blocks(LATE),) * 3, table, source, scratch=(chunks,))
    stacked = pltpu.VMEM((1, 3 * LATE // 2 * BLOCK, HALF), jnp.float32)
    return call(late_place_kernel, "place_late_blocks", f32(ROWS, WIDTH), table, before, *send_parts(parts), scratch=(stacked,))


def class_of(cols, groups, turn):
    return (cols + turn * groups) & (LAYERS - 1)


def choose_turn(filter_cols):
    turns = jnp.arange(LAYERS, dtype=jnp.int32)
    ones = jnp.left_shift(1, 8 * class_of(filter_cols, filter_cols >> 2, turns[:, None, None]))
    counts = jnp.sum(ones.reshape(LAYERS, N_WIDE, OWN, LAYERS, KEPT), axis=(2, 4))
    each = (counts[..., None] >> (8 * turns)) & 255
    most = jnp.max(jnp.where(turns[:, None] == turns, 0, each), axis=(1, 2, 3))
    least = jnp.min(most)
    return jnp.min(jnp.where(most == least, turns, LAYERS - 1)), least > FIRST


def halos(cross, inner):
    count = lax.axis_size("wide")
    over = [(i, (i + 1) % count if i % 2 else (i - 1) % count) for i in range(count)]
    return lax.ppermute(cross, "wide", over), lax.ppermute(inner, "wide", [(i, i ^ 1) for i in range(count)])


def tables(block_cols, filter_cols, wide_index, layer, turn):
    first_row = wide_index * OWN
    base = first_row - OWN

    def own(cols):
        mine = lax.dynamic_slice_in_dim(cols, first_row, OWN, 0)
        mine = (mine - base) & (NBR - 1)
        turned = lax.dynamic_slice_in_dim(jnp.concatenate([mine, mine], axis=1), layer * (KNZ // LAYERS), KNZ, 1)
        return mine, turned

    _, cols = own(block_cols)
    kept, kept_turned = own(filter_cols)
    places = jnp.arange(CLASS, dtype=jnp.int32)

    def classes(mine):
        return class_of(mine, (base >> 2) + (mine >> 2), turn)

    def at_place(mine):
        return jnp.where(classes(mine) == layer, mine >> 2, CLASS)

    slots = jnp.arange(KNZ, dtype=jnp.int32)
    slot = jnp.min(jnp.where(at_place(cols)[:, None, :] == places[None, :, None], slots, KNZ), axis=2)
    keep = jnp.max((at_place(kept)[:, None, :] == places[None, :, None]).astype(jnp.int32), axis=2)

    wanted = kept_turned.reshape(OWN, LAYERS, KEPT).transpose(1, 0, 2).reshape(LAYERS, MOST)
    groups = classes(wanted)
    here = groups == layer
    order = jnp.arange(MOST, dtype=jnp.int32)
    earlier = order[None, :] < order[:, None]
    rank = jnp.sum((here[:, None, :] & earlier).astype(jnp.int32), axis=2)
    code = (order >> 2) * OWN + (wanted >> 2)
    chosen = here[:, None, :] & (rank[:, None, :] == order[None, :, None])
    send = jnp.max(jnp.where(chosen, code[:, None, :], -1), axis=2)
    group = groups[0]
    source = (layer - group) & (LAYERS - 1)
    place = jnp.sum(((group[None, :] == group[:, None]) & earlier).astype(jnp.int32), axis=1)
    mine = source == 0
    first = jnp.where(mine, place, MOST + FIRST * (source - 1) + place)
    late = jnp.logical_not(mine) & (place >= FIRST)
    first = jnp.where(late, -1, first)
    late = jnp.where(late, LATE * (source - 1) + place - FIRST, -1)
    return jnp.concatenate([jnp.reshape(part, -1) for part in (cols, slot, keep, send, first, late, wide_index & 1)])


def local(restart, slab_slot, block_cols, filter_cols):
    wide_index = lax.axis_index("wide")
    layer = lax.axis_index("narrow")
    turn, late = choose_turn(filter_cols)
    table, late = lax.optimization_barrier((tables(block_cols, filter_cols, wide_index, layer, turn), late))

    packed = call(pack_kernel, "pack", f32(N_WIDE, 9, 1, 128), slab_slot, restart)
    arrived = lax.all_to_all(packed, "wide", split_axis=0, concat_axis=0, tiled=True)
    scratch = (pltpu.VMEM((8 * N_WIDE, 128), jnp.float32), pltpu.VMEM((N_WIDE, 128), jnp.float32)) + (pltpu.VMEM((ROWS, 128), jnp.float32),) * 2
    mine = call(unpack_kernel, "unpack", f32(ROWS, WIDTH), arrived, scratch=scratch, scalars=0)
    shards = (mine, shift(mine, "narrow", -1), shift(mine, "narrow", -2), shift(mine, "narrow", -3))

    half = f32(ROWS, WIDTH)
    whole = f32(ROWS, CLASS_COLS)
    sent = (blocks(MOST), blocks(FIRST), blocks(FIRST), blocks(FIRST))
    flops = 2 * 3 * ROWS * KNZ * BLOCK * CLASS_COLS
    chunks = pltpu.VMEM((2 * LAYERS, ROWS, HALF), jnp.float32)
    own, cross, inner = call(
        class_kernel, "columns_of_class", (whole, half, half), table, *shards, scratch=(chunks, RIGHT[2]), size=4 << 20
    )
    cross, inner = halos(cross, inner)

    square, cross_next, inner_next, *parts = call(
        square_kernel, "square", (whole, half, half) + sent, table, *shards, own, cross, inner,
        scratch=RIGHT, size=8 << 20, flops=flops,
    )
    cross, inner = halos(cross_next, inner_next)
    squared = place(table, parts[0], send_parts(parts[1:]))

    step, *parts = call(
        cubic_kernel, "cubic", (whole,) + sent, table, *shards, square, cross, inner, own,
        scratch=RIGHT, size=8 << 20, flops=flops,
    )
    updated = place(table, parts[0], send_parts(parts[1:]))

    def with_late(state):
        _, squared, updated = state
        return jnp.zeros((), bool), place_late(table, squared, square), place_late(table, updated, step)

    return lax.while_loop(lambda state: state[0], with_late, (late, squared, updated))[1:]


def solution(mesh):
    placed = (P("wide", "narrow"), P("wide"), P(), P())
    return jax.shard_map(
        local,
        mesh=mesh,
        in_specs=placed,
        out_specs=(P("wide", "narrow"), P("wide", "narrow")),
        check_vma=False,
    )
```

```python
import functools

import jax
import jax.numpy as jnp
from jax import lax
from jax.experimental import pallas as pl
from jax.experimental.pallas import tpu as pltpu
from jax.sharding import PartitionSpec as P

BLOCK = 64
KNZ = 16
JNZ = 16
SLAB = 4
N_WIDE = 128
LAYERS = 4
OWN = 8
NBR = 1024
SLABS = 128
ROWS = OWN * BLOCK
WIDTH = 256
CLASS = 6
CLASS_COLS = CLASS * BLOCK
NEAR = 3 * OWN
HALF = 2 * BLOCK
KEPT = JNZ // LAYERS
MOST = OWN * KEPT
FIRST = 18
LATE = MOST - FIRST

AT_ROW = 0
AT_SLOT = AT_ROW + OWN * KNZ
AT_KEEP = AT_SLOT + OWN * CLASS
AT_SEND = AT_KEEP + OWN * CLASS
AT_PLACE = AT_SEND + LAYERS * OWN * KEPT
AT_LATE = AT_PLACE + OWN * KEPT
AT_ODD = AT_LATE + OWN * KEPT

VMEM = pl.BlockSpec(memory_space=pltpu.VMEM)
SMEM = pl.BlockSpec(memory_space=pltpu.SMEM)
PARAMS = pltpu.CompilerParams(vmem_limit_bytes=24 * 1024 * 1024)


def cost(flops, bytes_accessed):
    return pl.CostEstimate(flops=flops, bytes_accessed=bytes_accessed, transcendentals=0)


def f32(*shape):
    return jax.ShapeDtypeStruct(shape, jnp.float32)


def pack_kernel(slot_ref, rows_ref, out_ref):
    low = lax.broadcasted_iota(jnp.int32, (8, 128), 0) < SLAB
    for pair in range(SLABS // 2):
        left = rows_ref[8 * pair : 8 * pair + 8, 0:128]
        right = rows_ref[8 * pair : 8 * pair + 8, 128:256]
        first = jnp.where(low, left, pltpu.roll(right, SLAB, 0))
        second = jnp.where(low, pltpu.roll(left, SLAB, 0), right)
        for which, tile in ((0, first), (1, second)):
            slot = slot_ref[2 * pair + which]
            target = slot >> 7
            out_ref[target, 0:8] = tile.reshape(8, 1, 128)
            out_ref[target, 8] = jnp.full((1, 128), (slot & 127).astype(jnp.float32))


def unpack_kernel(arrived_ref, rows_ref, tiles, places, *halves):
    for source in range(N_WIDE):
        tiles[8 * source : 8 * source + 8, :] = arrived_ref[source, 0:8].reshape(8, 128)
        places[source : source + 1, :] = arrived_ref[source, 8]
    order = lax.broadcasted_iota(jnp.int32, (SLABS, N_WIDE), 0).astype(jnp.float32)
    chosen = (jnp.transpose(places[...]) == order).astype(jnp.bfloat16)
    for row in range(8):
        rest = tiles[pl.ds(row, N_WIDE, stride=8), :]
        found = jnp.zeros((SLABS, 128), jnp.float32)
        for _ in range(3):
            part = rest.astype(jnp.bfloat16)
            rest = rest - part.astype(jnp.float32)
            found = found + jnp.dot(chosen, part, preferred_element_type=jnp.float32)
        half = row // SLAB
        halves[half][pl.ds(row % SLAB, SLABS, stride=SLAB), :] = found
    for half in range(2):
        rows_ref[:, half * 128 : (half + 1) * 128] = halves[half][...]


def pick(source, chunk, row, half, there, wanted, other=0.0):
    block = source[chunk, pl.ds(pl.multiple_of(row, BLOCK), BLOCK), :]
    return jnp.where(there, jnp.where(half == wanted, block, pltpu.roll(block, BLOCK, 1)), other)


def first_lanes():
    return lax.broadcasted_iota(jnp.int32, (BLOCK, HALF), 1) < BLOCK


def pack_blocks(table_ref, source, out_ref, at):
    first_half = first_lanes()

    def one(entry, wanted):
        there = entry >= 0
        place = entry & (OWN - 1)
        row = (jnp.maximum(entry, 0) >> 3) * BLOCK
        return pick(source, jnp.where(there, place >> 1, 0), row, place & 1, there, wanted)

    for pair in range(out_ref.shape[0] // BLOCK):
        block = jnp.where(first_half, one(table_ref[at + 2 * pair], 0), one(table_ref[at + 2 * pair + 1], 1))
        out_ref[pair * BLOCK : (pair + 1) * BLOCK, :] = block


def place_blocks(table_ref, source, out_ref, at, before=None):
    first_half = first_lanes()
    for i in range(OWN):
        rows = slice(i * BLOCK, (i + 1) * BLOCK)
        for c in range(KEPT // 2):
            cols = slice(c * HALF, (c + 1) * HALF)
            other = 0.0 if before is None else before[rows, cols]

            def one(entry, wanted):
                safe = jnp.maximum(entry, 0)
                return pick(source, 0, (safe >> 1) * BLOCK, safe & 1, entry >= 0, wanted, other)

            slot = at + i * KEPT + 2 * c
            out_ref[rows, cols] = jnp.where(first_half, one(table_ref[slot], 0), one(table_ref[slot + 1], 1))


def stack_blocks(parts, stacked):
    row = 0
    for part in parts:
        stacked[0, row : row + part.shape[0], :] = part[...]
        row += part.shape[0]


def place_kernel(table_ref, p0, p1, p2, p3, out_ref, stacked):
    stack_blocks((p0, p1, p2, p3), stacked)
    place_blocks(table_ref, stacked, out_ref, AT_PLACE)


def late_pack_kernel(table_ref, source_ref, o1, o2, o3, chunks):
    for q in range(CLASS // 2):
        chunks[q] = source_ref[:, q * HALF : (q + 1) * HALF]
    for r, out_ref in enumerate((o1, o2, o3)):
        pack_blocks(table_ref, chunks, out_ref, AT_SEND + (r + 1) * MOST + FIRST)


def late_place_kernel(table_ref, before_ref, p1, p2, p3, out_ref, stacked):
    stack_blocks((p1, p2, p3), stacked)
    place_blocks(table_ref, stacked, out_ref, AT_LATE, before_ref)


def write_halos(table_ref, source, cross_ref, inner_ref):
    odd = table_ref[AT_ODD]
    for q in range(2):
        cols = slice(q * HALF, (q + 1) * HALF)
        cross_ref[:, cols] = source[odd + q]
        inner_ref[:, cols] = source[1 - odd + q]


def class_kernel(table_ref, s0, s1, s2, s3, own_ref, cross_ref, inner_ref, chunks, mine):
    for r, shard in enumerate((s0, s1, s2, s3)):
        chunks[2 * r] = shard[:, 0:128]
        chunks[2 * r + 1] = shard[:, 128:256]
    first_half = first_lanes()
    for i in range(OWN):
        rows = slice(i * BLOCK, (i + 1) * BLOCK)

        def one(slot, wanted):
            there = slot != KNZ
            safe = jnp.where(there, slot, 0)
            return pick(chunks, safe >> 1, i * BLOCK, safe & 1, there, wanted)

        for q in range(CLASS // 2):
            at = AT_SLOT + i * CLASS + 2 * q
            block = jnp.where(first_half, one(table_ref[at], 0), one(table_ref[at + 1], 1))
            own_ref[rows, q * 128 : (q + 1) * 128] = block
            mine[q, rows, :] = block
    write_halos(table_ref, mine, cross_ref, inner_ref)


def split(x):
    high = x.astype(jnp.bfloat16)
    return high, (x - high.astype(jnp.float32)).astype(jnp.bfloat16)


def product(table_ref, shards, own_ref, cross, inner, right_high, right_low, finish):
    empty = jnp.zeros((ROWS, 128), jnp.bfloat16)
    odd = table_ref[AT_ODD]
    for source, side in ((cross, odd), (own_ref, None), (inner, 1 - odd)):
        for q in range(source.shape[1] // HALF):
            high, low = split(source[:, q * HALF : (q + 1) * HALF])
            if side is None:
                place = (slice(ROWS, 2 * ROWS), slice(q * HALF, (q + 1) * HALF))
            else:
                place = (
                    pl.ds(pl.multiple_of(side * 2 * ROWS, 2 * ROWS), ROWS),
                    pl.ds(pl.multiple_of((side + q) * HALF, HALF), HALF),
                )
            right_high[place] = high
            right_low[place] = low
    for store in (right_high, right_low):
        store[0:ROWS, WIDTH:CLASS_COLS] = empty
        store[2 * ROWS : 3 * ROWS, 0:128] = empty
    dot = functools.partial(jnp.dot, preferred_element_type=jnp.float32)
    for i in range(OWN):
        rows = slice(i * BLOCK, (i + 1) * BLOCK)
        total = jnp.zeros((BLOCK, CLASS_COLS), jnp.float32)
        for r, shard in enumerate(shards):
            high, low = split(shard[rows, :])
            places = [
                pl.ds(pl.multiple_of(table_ref[AT_ROW + i * KNZ + 4 * r + k] * BLOCK, BLOCK), BLOCK)
                for k in range(KNZ // LAYERS)
            ]
            weight_high = jnp.concatenate([right_high[p, :] for p in places], axis=0)
            weight_low = jnp.concatenate([right_low[p, :] for p in places], axis=0)
            both = dot(jnp.concatenate([high, low], axis=0), weight_high)
            total = total + both[:BLOCK] + both[BLOCK:] + dot(high, weight_low)
        finish(i, rows, total)


def square_kernel(
    table_ref, s0, s1, s2, s3, own_ref, cross, inner, square_ref, to_cross, to_inner, o0, o1, o2, o3, right_high, right_low, chunks
):
    first_half = first_lanes()

    def finish(i, rows, total):
        for q in range(CLASS // 2):
            at = AT_KEEP + i * CLASS + 2 * q
            keep = jnp.where(first_half, table_ref[at], table_ref[at + 1]) != 0
            block = jnp.where(keep, total[:, q * 128 : (q + 1) * 128], 0.0)
            chunks[q, rows, :] = block
            square_ref[rows, q * 128 : (q + 1) * 128] = block

    product(table_ref, (s0, s1, s2, s3), own_ref, cross, inner, right_high, right_low, finish)
    write_halos(table_ref, chunks, to_cross, to_inner)
    for r, out_ref in enumerate((o0, o1, o2, o3)):
        pack_blocks(table_ref, chunks, out_ref, AT_SEND + r * MOST)


def cubic_kernel(
    table_ref, s0, s1, s2, s3, own_ref, cross, inner, keep_ref, step_ref, o0, o1, o2, o3, right_high, right_low, chunks
):

    def finish(i, rows, total):
        for q in range(CLASS // 2):
            cols = slice(q * 128, (q + 1) * 128)
            block = 1.5 * keep_ref[rows, cols] - 0.5 * total[:, cols]
            chunks[q, rows, :] = block
            step_ref[rows, cols] = block

    product(table_ref, (s0, s1, s2, s3), own_ref, cross, inner, right_high, right_low, finish)
    for r, out_ref in enumerate((o0, o1, o2, o3)):
        pack_blocks(table_ref, chunks, out_ref, AT_SEND + r * MOST)


RIGHT = [
    pltpu.VMEM((NEAR * BLOCK, CLASS_COLS), jnp.bfloat16),
    pltpu.VMEM((NEAR * BLOCK, CLASS_COLS), jnp.bfloat16),
    pltpu.VMEM((CLASS // 2, ROWS, HALF), jnp.float32),
]


def shift(x, axis, by):
    count = lax.axis_size(axis)
    return lax.ppermute(x, axis, [(i, (i + by) % count) for i in range(count)])


def call(kernel, name, outs, *operands, scratch=(), size=1 << 20, flops=0, scalars=1):
    single = not isinstance(outs, tuple)
    return pl.pallas_call(
        kernel,
        out_shape=outs,
        in_specs=[SMEM] * scalars + [VMEM] * (len(operands) - scalars),
        out_specs=VMEM if single else (VMEM,) * len(outs),
        scratch_shapes=list(scratch),
        compiler_params=PARAMS,
        cost_estimate=cost(flops, size),
        name=name,
    )(*operands)


def blocks(count):
    return f32(count // 2 * BLOCK, HALF)


def send_parts(parts):
    near, far, back = parts
    near, back = shift(near, "narrow", 1), shift(back, "narrow", 3)
    return near, shift(far, "narrow", 2), back


def place(table, own, parts):
    stacked = pltpu.VMEM((1, (MOST + 3 * FIRST) // 2 * BLOCK, HALF), jnp.float32)
    return call(place_kernel, "place_blocks", f32(ROWS, WIDTH), table, own, *parts, scratch=(stacked,))


def place_late(table, before, source):
    chunks = pltpu.VMEM((CLASS // 2, ROWS, HALF), jnp.float32)
    parts = call(late_pack_kernel, "late_blocks", (blocks(LATE),) * 3, table, source, scratch=(chunks,))
    stacked = pltpu.VMEM((1, 3 * LATE // 2 * BLOCK, HALF), jnp.float32)
    return call(late_place_kernel, "place_late_blocks", f32(ROWS, WIDTH), table, before, *send_parts(parts), scratch=(stacked,))


def any_late(filter_cols):
    ones = jnp.left_shift(1, 8 * (filter_cols & (LAYERS - 1)))
    counts = jnp.sum(ones.reshape(N_WIDE, OWN, LAYERS, KEPT), axis=(1, 3))
    layers = jnp.arange(LAYERS, dtype=jnp.int32)
    each = (counts[:, :, None] >> (8 * layers)) & 255
    return jnp.max(jnp.where(layers[:, None] == layers, 0, each)) > FIRST


def halos(cross, inner):
    count = lax.axis_size("wide")
    over = [(i, (i + 1) % count if i % 2 else (i - 1) % count) for i in range(count)]
    return lax.ppermute(cross, "wide", over), lax.ppermute(inner, "wide", [(i, i ^ 1) for i in range(count)])


def tables(block_cols, filter_cols, wide_index, layer):
    first_row = wide_index * OWN
    base = first_row - OWN

    def own(cols):
        mine = lax.dynamic_slice_in_dim(cols, first_row, OWN, 0)
        mine = (mine - base) & (NBR - 1)
        turned = lax.dynamic_slice_in_dim(jnp.concatenate([mine, mine], axis=1), layer * (KNZ // LAYERS), KNZ, 1)
        return mine, turned

    _, cols = own(block_cols)
    kept, kept_turned = own(filter_cols)
    places = layer + LAYERS * jnp.arange(CLASS, dtype=jnp.int32)
    slots = jnp.arange(KNZ, dtype=jnp.int32)
    slot = jnp.min(jnp.where(cols[:, None, :] == places[None, :, None], slots, KNZ), axis=2)
    keep = jnp.max((kept[:, None, :] == places[None, :, None]).astype(jnp.int32), axis=2)

    wanted = kept_turned.reshape(OWN, LAYERS, KEPT).transpose(1, 0, 2).reshape(LAYERS, MOST)
    here = (wanted & (LAYERS - 1)) == layer
    order = jnp.arange(MOST, dtype=jnp.int32)
    earlier = order[None, :] < order[:, None]
    rank = jnp.sum((here[:, None, :] & earlier).astype(jnp.int32), axis=2)
    code = (order >> 2) * OWN + ((wanted - layer) >> 2)
    chosen = here[:, None, :] & (rank[:, None, :] == order[None, :, None])
    send = jnp.max(jnp.where(chosen, code[:, None, :], -1), axis=2)
    group = wanted[0] & (LAYERS - 1)
    source = (layer - group) & (LAYERS - 1)
    place = jnp.sum(((group[None, :] == group[:, None]) & earlier).astype(jnp.int32), axis=1)
    mine = source == 0
    first = jnp.where(mine, place, MOST + FIRST * (source - 1) + place)
    late = jnp.logical_not(mine) & (place >= FIRST)
    first = jnp.where(late, -1, first)
    late = jnp.where(late, LATE * (source - 1) + place - FIRST, -1)
    return jnp.concatenate([jnp.reshape(part, -1) for part in (cols, slot, keep, send, first, late, wide_index & 1)])


def local(restart, slab_slot, block_cols, filter_cols):
    wide_index = lax.axis_index("wide")
    layer = lax.axis_index("narrow")
    table, late = lax.optimization_barrier((tables(block_cols, filter_cols, wide_index, layer), any_late(filter_cols)))

    packed = call(pack_kernel, "pack", f32(N_WIDE, 9, 1, 128), slab_slot, restart)
    arrived = lax.all_to_all(packed, "wide", split_axis=0, concat_axis=0, tiled=True)
    scratch = (pltpu.VMEM((8 * N_WIDE, 128), jnp.float32), pltpu.VMEM((N_WIDE, 128), jnp.float32)) + (pltpu.VMEM((ROWS, 128), jnp.float32),) * 2
    mine = call(unpack_kernel, "unpack", f32(ROWS, WIDTH), arrived, scratch=scratch, scalars=0)
    after, before = shift(mine, "narrow", -1), shift(mine, "narrow", -3)
    shards = (mine, after, shift(mine, "narrow", -2), before)

    half = f32(ROWS, WIDTH)
    whole = f32(ROWS, CLASS_COLS)
    sent = (blocks(MOST), blocks(FIRST), blocks(FIRST), blocks(FIRST))
    flops = 2 * 3 * ROWS * KNZ * BLOCK * CLASS_COLS
    chunks = pltpu.VMEM((2 * LAYERS, ROWS, HALF), jnp.float32)
    own, cross, inner = call(
        class_kernel, "columns_of_class", (whole, half, half), table, *shards, scratch=(chunks, RIGHT[2]), size=4 << 20
    )
    cross, inner = halos(cross, inner)

    square, cross_next, inner_next, *parts = call(
        square_kernel, "square", (whole, half, half) + sent, table, *shards, own, cross, inner,
        scratch=RIGHT, size=8 << 20, flops=flops,
    )
    cross, inner = halos(cross_next, inner_next)
    squared = place(table, parts[0], send_parts(parts[1:]))

    step, *parts = call(
        cubic_kernel, "cubic", (whole,) + sent, table, *shards, square, cross, inner, own,
        scratch=RIGHT, size=8 << 20, flops=flops,
    )
    updated = place(table, parts[0], send_parts(parts[1:]))

    def with_late(state):
        _, squared, updated = state
        return jnp.zeros((), bool), place_late(table, squared, square), place_late(table, updated, step)

    return lax.while_loop(lambda state: state[0], with_late, (late, squared, updated))[1:]


def solution(mesh):
    placed = (P("wide", "narrow"), P("wide"), P(), P())
    return jax.shard_map(
        local,
        mesh=mesh,
        in_specs=placed,
        out_specs=(P("wide", "narrow"), P("wide", "narrow")),
        check_vma=False,
    )
```
